768 devices in a mesh: gx: 64 (over x, y, core), gy: 12 (over z).
Axes of the slice: x: 4, y: 8, z: 12, core: 2. Of those that a mesh axis runs over, the one named last changes fastest.
Arguments:
- right_side: float32 [3, 256, 96, 256], P(None, 'gx', 'gy'), may hold values from -24 to 24
- block_matrix: float32 [3, 3, 256, 96, 256], P(None, None, 'gx', 'gy'), may hold values from -1 to 8, as said below
- mobility: float32 [3, 256, 96, 256], P(None, 'gx', 'gy'), may hold values from 0.2 to 1
- trans: float32 [6, 256, 96, 256], P(None, 'gx', 'gy'), may hold values from 0.02 to 1
- active_mask: int32 [256, 96, 256], P('gx', 'gy'), may hold values 0 or 1
- cell_map: int32 [256, 96, 256], P('gx', 'gy'), may hold values from 0 to 63
- coarse_owner: int32 [64, 12], P('gx', 'gy'), may hold values from 0 to 11, each once within a row
- coarse_rows: float32 [49152, 768], P(('gx', 'gy')), may hold values from -0.109375 to 0.109375
Outputs:
- solution: float32 [3, 256, 96, 256], P(None, 'gx', 'gy')
The draws below stay inside these ranges and needn't reach their ends.
Inputs may be any that keep to these rules, and one draw needn't show every extreme that they name: `coarse_owner`: each row holds every rank of 0 to 11 once. `block_matrix`: each cell's block has a positive diagonal, a positive first column, and is strictly diagonally dominant by rows.
All inputs are finite; a program needn't handle non-finite values. No bound on the sum of `active_mask` on one device may be relied on, other than what follows from the above.
Results may differ from the reference program's by a relative error of at most 0.0065.
Values sent between devices are 32-bit elements; how exact they have to be, the bound alone decides.
No kernel may reach another device: no remote copies, remote signals or barrier semaphores. Data moves between devices by JAX's collectives and lax.ppermute only.
A program may use at most 32 MiB of HBM per device.

```python
import math
import jax
import jax.numpy as jnp
import numpy as np
from jax import lax

C1 = 4
C2 = 8
CZ = 256
NCL = 64
SMOOTH = 2
NX = 256
NY = 96
NZ = 256
BLOCKS_X = 64
BLOCKS_Y = 12
GROUP_CELLS = 98304
GROUP_COARSE = 768
COARSE_ROWS = 49152
N_GX = 64
N_GY = 12


lower_table = np.array([[4.0, -1.0, -1.0], [0.2, 3.0, -1.0], [0.2, -1.0, 3.0]], np.float32)


upper_table = np.array([[8.0, 1.0, 1.0], [1.0, 6.0, 1.0], [1.0, 1.0, 6.0]], np.float32)


def draw_block_matrix(key, part):
    key = jax.random.fold_in(key, 17)
    unit = jax.random.uniform(key, (3, 3, NX, NY, NZ), jnp.float32)
    low = jnp.asarray(lower_table).reshape(3, 3, 1, 1, 1)
    high = jnp.asarray(upper_table).reshape(3, 3, 1, 1, 1)
    return (low + (high - low) * unit).astype(jnp.float32)


def touch_ends(values, key, smallest, high):
    longest = values.shape.index(max(values.shape))
    spots = []
    for shift in (0, 1):
        where = [jax.random.randint(jax.random.fold_in(key, axis), (), 0, length) for axis, length in enumerate(values.shape)]
        where[longest] = (where[longest] + shift) % values.shape[longest]
        spots.append(tuple(where))
    return values.at[spots[0]].set(smallest).at[spots[1]].set(high)


def block_levels(key, extent, shards, low, top_value):
    def one(dim, parts):
        heights = jax.random.uniform(jax.random.fold_in(jax.random.fold_in(key, 6), dim), (parts,), jnp.float32, low / len(shards), top_value / len(shards))
        return jnp.repeat(jnp.exp(heights), extent[dim] // parts).reshape((-1,) + (1,) * (len(extent) - dim - 1))

    gain = one(*shards[0])
    for cut in shards[1:]:
        gain = gain * one(*cut)
    return gain


def noise(own_key, extent, spread, bound, pieces=(), kind=jnp.bfloat16):
    entries = spread * jax.random.normal(own_key, extent, jnp.float32)
    if pieces:
        entries = entries * block_levels(own_key, extent, pieces, -0.22, 0.18)
    return jnp.clip(entries, -bound, bound).astype(kind)


def setup_inputs(seed: int = 0) -> dict:
    key_of = jax.random.split(jax.random.key(seed), 9)
    return {
        "right_side": noise(key_of[0], (3, NX, NY, NZ), 4.0, 24.0, ((1, 64), (2, 12)), jnp.float32),
        "block_matrix": draw_block_matrix(jax.random.fold_in(key_of[8], 71), 0),
        "mobility": jnp.clip(jnp.exp(math.log(1.0) - 1.609438 * jax.random.uniform(key_of[2], (3, NX, NY, NZ), jnp.float32) ** block_levels(key_of[2], (3, NX, NY, NZ), ((1, 64), (2, 12)), -0.2, 0.2)), 0.2, 1.0),
        "trans": jnp.clip(jnp.exp(math.log(1.0) - 3.912023 * jax.random.uniform(key_of[3], (6, NX, NY, NZ), jnp.float32) ** block_levels(key_of[3], (6, NX, NY, NZ), ((1, 64), (2, 12)), -0.2, 0.2)), 0.02, 1.0),
        "active_mask": touch_ends((jax.random.randint(key_of[4], (NX, NY, NZ), 0, 4) < 3).astype(jnp.int32), jax.random.fold_in(key_of[4], 1), 0, 1),
        "cell_map": touch_ends(jax.random.randint(key_of[5], (NX, NY, NZ), 0, NCL), jax.random.fold_in(key_of[5], 1), 0, NCL - 1).astype(jnp.int32),
        "coarse_owner": jax.vmap(lambda own: jax.random.permutation(own, BLOCKS_Y))(jax.random.split(key_of[6], BLOCKS_X)).reshape((BLOCKS_X, BLOCKS_Y)).astype(jnp.int32),
        "coarse_rows": noise(key_of[7], (COARSE_ROWS, GROUP_COARSE), (GROUP_CELLS // 32) ** -0.5, 0.109375, ((0, 768),), jnp.float32),
    }


damping = 0.8


def face_sum(quantity, coefficients):
    pad_width = [(0, 0)] * (quantity.ndim - 3) + [(1, 1), (1, 1), (1, 1)]
    padded = jnp.pad(quantity, pad_width)
    neighbours = (padded[..., 2:, 1:-1, 1:-1], padded[..., :-2, 1:-1, 1:-1],
                  padded[..., 1:-1, 2:, 1:-1], padded[..., 1:-1, :-2, 1:-1],
                  padded[..., 1:-1, 1:-1, 2:], padded[..., 1:-1, 1:-1, :-2])
    running = coefficients[0] * neighbours[0]
    for side_index in range(1, 6):
        running = running + coefficients[side_index] * neighbours[side_index]
    return running


def block_inverse(matrix, mask_float):
    entry = [[mask_float * matrix[row_index, col_index] + (1.0 - mask_float) * (1.0 if row_index == col_index else 0.0)
              for col_index in range(3)] for row_index in range(3)]
    cof_00 = entry[1][1] * entry[2][2] - entry[1][2] * entry[2][1]
    cof_01 = -(entry[1][0] * entry[2][2] - entry[1][2] * entry[2][0])
    cof_02 = entry[1][0] * entry[2][1] - entry[1][1] * entry[2][0]
    cof_10 = -(entry[0][1] * entry[2][2] - entry[0][2] * entry[2][1])
    cof_11 = entry[0][0] * entry[2][2] - entry[0][2] * entry[2][0]
    cof_12 = -(entry[0][0] * entry[2][1] - entry[0][1] * entry[2][0])
    cof_20 = entry[0][1] * entry[1][2] - entry[0][2] * entry[1][1]
    cof_21 = -(entry[0][0] * entry[1][2] - entry[0][2] * entry[1][0])
    cof_22 = entry[0][0] * entry[1][1] - entry[0][1] * entry[1][0]
    determinant = entry[0][0] * cof_00 + entry[0][1] * cof_01 + entry[0][2] * cof_02
    recip = 1.0 / determinant
    return jnp.stack([jnp.stack([cof_00 * recip, cof_10 * recip, cof_20 * recip]),
                      jnp.stack([cof_01 * recip, cof_11 * recip, cof_21 * recip]),
                      jnp.stack([cof_02 * recip, cof_12 * recip, cof_22 * recip])])


def to_blocks(values):
    return values.reshape(N_GX, C1, N_GY, C2, CZ).transpose(0, 2, 1, 3, 4).reshape(N_GX * N_GY, C1 * C2 * CZ)


def from_blocks(values):
    return values.reshape(N_GX, N_GY, C1, C2, CZ).transpose(0, 2, 1, 3, 4).reshape(NX, NY, NZ)


def reference(right_side, block_matrix, mobility, trans, active_mask, cell_map, coarse_owner, coarse_rows):
    mask_float = active_mask.astype(jnp.float32)
    mob_total = mobility[0] + mobility[1] + mobility[2]
    coupling = (mask_float * mob_total)[None] * trans
    diag_p = mask_float * (block_matrix[0, 0] + block_matrix[1, 0] + block_matrix[2, 0]) + (1.0 - mask_float)
    inv_diag = 1.0 / diag_p
    inverse = block_inverse(block_matrix, mask_float)
    block_ids = (jnp.arange(N_GX * N_GY, dtype=jnp.int32) * NCL)[:, None]
    segment_ids = (to_blocks(cell_map).astype(jnp.int32) + block_ids).reshape(-1)
    row_blocks = coarse_rows.reshape(N_GX, N_GY, NCL, N_GY * NCL)
    owner_index = jnp.broadcast_to(coarse_owner.astype(jnp.int32)[:, :, None], (N_GX, N_GY, NCL))

    def operate(field_in):
        neighbour = face_sum(mask_float[None] * field_in, trans)
        row_list = []
        for row_index in range(3):
            direct = (block_matrix[row_index, 0] * field_in[0] + block_matrix[row_index, 1] * field_in[1]
                      + block_matrix[row_index, 2] * field_in[2])
            flux_sum = neighbour[0] if row_index == 0 else neighbour[0] + neighbour[row_index]
            row_list.append(mask_float * (direct - mobility[row_index] * flux_sum) + (1.0 - mask_float) * field_in[row_index])
        return jnp.stack(row_list)

    def precondition(residual_in):
        pressure_rhs = residual_in[0] + residual_in[1] + residual_in[2]
        coarse_sums = jax.ops.segment_sum(to_blocks(pressure_rhs).reshape(-1), segment_ids,
                                          num_segments=N_GX * N_GY * NCL).reshape(N_GX, N_GY * NCL)
        owned = jnp.einsum('abkm,am->abk', row_blocks, coarse_sums, precision=lax.Precision.HIGHEST)
        chosen = jnp.take_along_axis(owned, owner_index, axis=1)
        pressure = from_blocks(chosen.reshape(-1)[segment_ids])
        for sweep_index in range(SMOOTH):
            pressure = pressure + damping * inv_diag * (pressure_rhs - diag_p * pressure
                                                        + face_sum(mask_float * pressure, coupling))
        neighbour = face_sum(mask_float * pressure, trans)
        second = []
        for row_index in range(3):
            applied = mask_float * (block_matrix[row_index, 0] * pressure - mobility[row_index] * neighbour)
            if row_index == 0:
                applied = applied + (1.0 - mask_float) * pressure
            second.append(residual_in[row_index] - applied)
        result = []
        for row_index in range(3):
            smoothed = (inverse[row_index, 0] * second[0] + inverse[row_index, 1] * second[1]
                        + inverse[row_index, 2] * second[2])
            result.append(pressure + smoothed if row_index == 0 else smoothed)
        return jnp.stack(result)

    first_z = precondition(right_side)
    first_w = operate(first_z)
    second_z = precondition(first_w)
    second_w = operate(second_z)
    gram_one = jnp.sum(first_w * first_w)
    gram_cross = jnp.sum(first_w * second_w)
    gram_two = jnp.sum(second_w * second_w)
    proj_one = jnp.sum(first_w * right_side)
    proj_two = jnp.sum(second_w * right_side)
    determinant = gram_one * gram_two - gram_cross * gram_cross
    coeff_one = (gram_two * proj_one - gram_cross * proj_two) / determinant
    coeff_two = (gram_one * proj_two - gram_cross * proj_one) / determinant
    return coeff_one * first_z + coeff_two * second_z
```

```python
import jax
import jax.numpy as jnp
from jax import lax
from jax.sharding import PartitionSpec as P

SMOOTH = 2


damping = 0.8


def face_values(padded):
    centre = padded[..., 1:-1, 1:-1, :]
    zero_rim = jnp.zeros_like(centre[..., :1])
    return (
        padded[..., 2:, 1:-1, :],
        padded[..., :-2, 1:-1, :],
        padded[..., 1:-1, 2:, :],
        padded[..., 1:-1, :-2, :],
        jnp.concatenate([centre[..., 1:], zero_rim], -1),
        jnp.concatenate([zero_rim, centre[..., :-1]], -1),
    )


def neighbour_sum(padded, coefficients):
    neighbours = face_values(padded)
    running = coefficients[0] * neighbours[0]
    for side_index in range(1, 6):
        running = running + coefficients[side_index] * neighbours[side_index]
    return running


def faces(field_in):
    received = []
    for axis, dim in (("gx", 1), ("gy", 2)):
        count = lax.axis_size(axis)
        ends = count - 1
        head = lax.slice_in_dim(field_in, 0, 1, axis=dim)
        tail = lax.slice_in_dim(field_in, field_in.shape[dim] - 1, field_in.shape[dim], axis=dim)
        received.append(lax.ppermute(tail, axis, [(i, i + 1) for i in range(ends)]))
        received.append(lax.ppermute(head, axis, [(i + 1, i) for i in range(ends)]))
    low_x, high_x, low_y, high_y = received
    pad = [(0, 0), (1, 1), (0, 0), (0, 0)]
    middle = jnp.concatenate([low_x, field_in, high_x], 1)
    return jnp.concatenate([jnp.pad(low_y, pad), middle, jnp.pad(high_y, pad)], 2)


def everyone(values, axis):
    count = lax.axis_size(axis)
    spread = jnp.broadcast_to(values[None, None], (count, 1) + values.shape)
    return lax.all_to_all(spread, axis, 0, 0)[:, 0]


def block_inverse(matrix, mask_float):
    entry = [
        [
            mask_float * matrix[row_index, col_index]
            + (1.0 - mask_float) * (1.0 if row_index == col_index else 0.0)
            for col_index in range(3)
        ]
        for row_index in range(3)
    ]
    cof_00 = entry[1][1] * entry[2][2] - entry[1][2] * entry[2][1]
    cof_01 = -(entry[1][0] * entry[2][2] - entry[1][2] * entry[2][0])
    cof_02 = entry[1][0] * entry[2][1] - entry[1][1] * entry[2][0]
    cof_10 = -(entry[0][1] * entry[2][2] - entry[0][2] * entry[2][1])
    cof_11 = entry[0][0] * entry[2][2] - entry[0][2] * entry[2][0]
    cof_12 = -(entry[0][0] * entry[2][1] - entry[0][1] * entry[2][0])
    cof_20 = entry[0][1] * entry[1][2] - entry[0][2] * entry[1][1]
    cof_21 = -(entry[0][0] * entry[1][2] - entry[0][2] * entry[1][0])
    cof_22 = entry[0][0] * entry[1][1] - entry[0][1] * entry[1][0]
    determinant = entry[0][0] * cof_00 + entry[0][1] * cof_01 + entry[0][2] * cof_02
    recip = 1.0 / determinant
    return jnp.stack(
        [
            jnp.stack([cof_00 * recip, cof_10 * recip, cof_20 * recip]),
            jnp.stack([cof_01 * recip, cof_11 * recip, cof_21 * recip]),
            jnp.stack([cof_02 * recip, cof_12 * recip, cof_22 * recip]),
        ]
    )


def on_device(
    right_side, block_matrix, mobility, trans, active_mask, cell_map, coarse_owner, coarse_rows
):
    highest = lax.Precision.HIGHEST
    mask_float = active_mask.astype(jnp.float32)
    mob_total = mobility[0] + mobility[1] + mobility[2]
    coupling = (mask_float * mob_total)[None] * trans
    diag_p = mask_float * (block_matrix[0, 0] + block_matrix[1, 0] + block_matrix[2, 0]) + (
        1.0 - mask_float
    )
    inv_diag = 1.0 / diag_p
    inverse = block_inverse(block_matrix, mask_float)
    aggregates = coarse_rows.shape[0]
    group_size = lax.axis_size("gy")
    onehot = (
        cell_map.reshape(-1)[None, :] == jnp.arange(aggregates, dtype=jnp.int32)[:, None]
    ).astype(jnp.float32)
    owner_pick = (jnp.arange(group_size, dtype=jnp.int32) == coarse_owner[0, 0]).astype(jnp.float32)

    def operate(field_in):
        neighbour = neighbour_sum(faces(mask_float[None] * field_in), trans)
        row_list = []
        for row_index in range(3):
            direct = (
                block_matrix[row_index, 0] * field_in[0]
                + block_matrix[row_index, 1] * field_in[1]
                + block_matrix[row_index, 2] * field_in[2]
            )
            flux_sum = neighbour[0] if row_index == 0 else neighbour[0] + neighbour[row_index]
            row_list.append(
                mask_float * (direct - mobility[row_index] * flux_sum)
                + (1.0 - mask_float) * field_in[row_index]
            )
        return jnp.stack(row_list)

    def precondition(residual_in):
        pressure_rhs = residual_in[0] + residual_in[1] + residual_in[2]
        coarse_local = jnp.dot(onehot, pressure_rhs.reshape(-1), precision=highest)
        coarse_all = everyone(coarse_local, "gy").reshape(-1)
        owned = jnp.dot(coarse_rows, coarse_all, precision=highest)
        returned = everyone(owned, "gy")
        own_values = jnp.dot(owner_pick, returned, precision=highest)
        pressure = jnp.dot(own_values, onehot, precision=highest).reshape(pressure_rhs.shape)
        for sweep_index in range(SMOOTH):
            padded = faces((mask_float * pressure)[None])[0]
            pressure = pressure + damping * inv_diag * (
                pressure_rhs - diag_p * pressure + neighbour_sum(padded, coupling)
            )
        neighbour = neighbour_sum(faces((mask_float * pressure)[None])[0], trans)
        second = []
        for row_index in range(3):
            applied = mask_float * (
                block_matrix[row_index, 0] * pressure - mobility[row_index] * neighbour
            )
            if row_index == 0:
                applied = applied + (1.0 - mask_float) * pressure
            second.append(residual_in[row_index] - applied)
        result = []
        for row_index in range(3):
            smoothed = (
                inverse[row_index, 0] * second[0]
                + inverse[row_index, 1] * second[1]
                + inverse[row_index, 2] * second[2]
            )
            result.append(pressure + smoothed if row_index == 0 else smoothed)
        return jnp.stack(result)

    first_z = precondition(right_side)
    first_w = operate(first_z)
    second_z = precondition(first_w)
    second_w = operate(second_z)
    sums = jnp.stack(
        [
            jnp.sum(first_w * first_w),
            jnp.sum(first_w * second_w),
            jnp.sum(second_w * second_w),
            jnp.sum(first_w * right_side),
            jnp.sum(second_w * right_side),
        ]
    )
    sums = jnp.sum(everyone(sums, "gx"), 0)
    sums = jnp.sum(everyone(sums, "gy"), 0)
    gram_one, gram_cross, gram_two, proj_one, proj_two = [sums[i] for i in range(5)]
    determinant = gram_one * gram_two - gram_cross * gram_cross
    coeff_one = (gram_two * proj_one - gram_cross * proj_two) / determinant
    coeff_two = (gram_one * proj_two - gram_cross * proj_one) / determinant
    return coeff_one * first_z + coeff_two * second_z


def solution(mesh):
    in_specs = (
        P(None, "gx", "gy", None),
        P(None, None, "gx", "gy", None),
        P(None, "gx", "gy", None),
        P(None, "gx", "gy", None),
        P("gx", "gy", None),
        P("gx", "gy", None),
        P("gx", "gy"),
        P(("gx", "gy"), None),
    )
    out_specs = P(None, "gx", "gy", None)
    return jax.shard_map(
        on_device, mesh=mesh, in_specs=in_specs, out_specs=out_specs, check_vma=False
    )
```

```python
import functools

import jax
import jax.numpy as jnp
from jax import lax
from jax.experimental import pallas as pl
from jax.experimental.pallas import tpu as pltpu
from jax.sharding import PartitionSpec as P

DAMPING = 0.8
F32 = jnp.float32
XO = 4
ROWS = 8
NC = 64

X_FIELD, X_VEM, X_CORNER, X_CELL13, X_CELL2, X_COARSE, X_TILES = 4, 28, 37, 45, 46, 47, 49
Y_FIELD, Y_VEM, Y_TILES = 2, 18, 23
X2_S, X2_COARSE, X2_TILES = 3, 6, 8
Y2_V, Y2_TILES = 4, 6
Y2_PLACES = (0, 1, 2, 3, 4, 5, 10, 11)


def row_index():
    return lax.broadcasted_iota(jnp.int32, (ROWS, 256), 0)


def turned(tile, by):
    return pltpu.roll(tile, by, axis=0)


def put(ref, index, tile):
    ref[8 * index : 8 * index + 8, :] = tile


def get(ref, index):
    return ref[8 * index : 8 * index + 8, :]


class Own:
    def __init__(self, place, block_ref, mobility_ref, mask_ref):
        self.mask = mask = mask_ref[place].astype(F32)
        self.rest = rest = 1.0 - mask
        self.block = [[block_ref[c, j, place] for j in range(3)] for c in range(3)]
        self.mobility = [mobility_ref[c, place] for c in range(3)]
        e = [
            [mask * self.block[c][j] + rest if c == j else mask * self.block[c][j] for j in range(3)]
            for c in range(3)
        ]
        cof = [
            [
                e[(c + 1) % 3][(j + 1) % 3] * e[(c + 2) % 3][(j + 2) % 3]
                - e[(c + 1) % 3][(j + 2) % 3] * e[(c + 2) % 3][(j + 1) % 3]
                for j in range(3)
            ]
            for c in range(3)
        ]
        recip = 1.0 / (e[0][0] * cof[0][0] + e[0][1] * cof[0][1] + e[0][2] * cof[0][2])
        self.inverse = [[cof[j][c] * recip for j in range(3)] for c in range(3)]
        self.entry = e
        self.scale = DAMPING * mask / (mask * (self.block[0][0] + self.block[1][0] + self.block[2][0]) + rest)

    def solve(self, vector):
        i = self.inverse
        return [i[c][0] * vector[0] + i[c][1] * vector[1] + i[c][2] * vector[2] for c in range(3)]

    def kappa(self):
        return self.scale * (self.mobility[0] + self.mobility[1] + self.mobility[2])

    def of_pressure(self):
        column = self.solve([self.entry[j][0] for j in range(3)])
        return [1.0 - column[0], -column[1], -column[2]]

    def of_flux(self):
        return self.solve([self.mask * self.mobility[j] for j in range(3)])


def cell_code(place, mask_ref, cell_ref):
    return jnp.where(mask_ref[place] > 0, cell_ref[place], -1).astype(F32)


def coarse_sums(cell_ref, of_row):
    wanted = lax.broadcasted_iota(jnp.int32, (NC, 256), 0)
    total = jnp.zeros((NC, 256), F32)
    for place in range(XO):
        cells, values = cell_ref[place], of_row(place)
        for row in range(ROWS):
            here = jnp.broadcast_to(cells[row : row + 1], (NC, 256)) == wanted
            total = total + jnp.where(here, jnp.broadcast_to(values[row : row + 1], (NC, 256)), 0.0)
    return jnp.sum(total[:, :128] + total[:, 128:], axis=1, keepdims=True)


def coarse_terms(sums, columns_ref, terms_ref, group):
    lane = lax.broadcasted_iota(jnp.int32, (NC // 2, 128), 1)
    weights = jnp.where(
        lane < NC,
        jnp.broadcast_to(sums[: NC // 2], (NC // 2, 128)),
        jnp.broadcast_to(sums[NC // 2 :], (NC // 2, 128)),
    )
    result = jnp.zeros(terms_ref.shape, F32)
    for j in range(group):
        terms_ref[j : j + 1, :] = columns_ref[j, NC // 2 : NC // 2 + 1, :]
    owners = terms_ref[...]
    for j in range(group):
        line = jnp.sum(columns_ref[j, : NC // 2, :] * weights, axis=0, keepdims=True)
        line = line + pltpu.roll(line, NC, axis=1)
        result = result + jnp.where(owners == float(j), jnp.broadcast_to(line, result.shape), 0.0)
    return result


def shifted_lanes(tile):
    lane = lax.broadcasted_iota(jnp.int32, (ROWS, 256), 1)
    after = jnp.where(lane < 255, pltpu.roll(tile, 255, axis=1), 0.0)
    before = jnp.where(lane > 0, pltpu.roll(tile, 1, axis=1), 0.0)
    return after, before


def flux(field, trans, place, tiles):
    own, halo = field(place, 0), field(place, 1)
    inner = row_index() < 7
    outer = row_index() > 0
    own_up, halo_up, own_down, halo_down = turned(own, 7), turned(halo, 7), turned(own, 1), turned(halo, 1)
    result = []
    for tile in tiles:
        if tile == 0:
            up, down = jnp.where(inner, own_up, halo_up), jnp.where(outer, own_down, halo_down)
        else:
            up, down = jnp.where(inner, halo_up, own_up), jnp.where(outer, halo_down, own_down)
        after, before = shifted_lanes(halo if tile else own)
        total = trans(0, place, tile) * field((place + 1) % 12, tile)
        total = total + trans(1, place, tile) * field((place + 11) % 12, tile)
        total = total + trans(2, place, tile) * up
        total = total + trans(3, place, tile) * down
        total = total + trans(4, place, tile) * after
        total = total + trans(5, place, tile) * before
        result.append(total)
    return result


def paired(tiles, to_next):
    first, second = tiles
    low = row_index() < 4
    if to_next:
        return jnp.where(low, turned(first, 4), second)
    return jnp.where(low, first, turned(second, 4))


def halo_tile(next_pair, previous_pair, which):
    low = row_index() < 4
    if which == 0:
        return jnp.where(low, next_pair, turned(previous_pair, 4))
    return jnp.where(low, turned(next_pair, 4), previous_pair)


def pack_kernel(
    group, owner_ref, rows_ref, right_ref, block_ref, mobility_ref, trans_ref, mask_ref, cell_ref,
    columns_ref, up_ref, down_ref, field_ref,
):
    lane = lax.broadcasted_iota(jnp.int32, (NC // 2, 128), 1)
    owner = jnp.full((8, 128), owner_ref[0, 0], jnp.int32).astype(F32)
    for pair in range(group // 2):
        part = rows_ref[:, 128 * pair : 128 * pair + 128]
        flipped = jnp.concatenate([part, part], axis=0).T
        for odd in range(2):
            block = flipped[NC * odd : NC * odd + NC]
            columns_ref[2 * pair + odd, : NC // 2, :] = jnp.where(lane < NC, block[: NC // 2], block[NC // 2 :])
            columns_ref[2 * pair + odd, NC // 2 :, :] = owner
    for out_ref in (up_ref, down_ref):
        out_ref[8 * Y_TILES - 4 :, :] = jnp.zeros((4, 256), F32)
    for half in range(2):
        cells, fields = [], []
        for place in (2 * half, 2 * half + 1):
            own = Own(place, block_ref, mobility_ref, mask_ref)
            cells.append(cell_code(place, mask_ref, cell_ref))
            right = [right_ref[c, place] for c in range(3)]
            fields.append(
                [trans_ref[face, place] for face in range(6)]
                + [own.kappa(), own.scale * (right[0] + right[1] + right[2])]
            )
            vem = [own.mask * v for v in own.solve(right)] + own.of_pressure() + own.of_flux()
            for f in range(9):
                field_ref[...] = vem[f]
                spot = 8 * Y_VEM + 4 * f + place
                up_ref[spot : spot + 1, :] = field_ref[7:8, :]
                down_ref[spot : spot + 1, :] = field_ref[0:1, :]
        for out_ref, to_next in ((up_ref, True), (down_ref, False)):
            put(out_ref, half, paired(cells, to_next))
            for k in range(8):
                put(out_ref, Y_FIELD + 2 * k + half, paired([fields[0][k], fields[1][k]], to_next))


def y_halo(next_ref, previous_ref, index, place):
    at = index + place // 2
    return halo_tile(get(next_ref, at), get(previous_ref, at), place % 2)


def sides_kernel(
    group, right_ref, block_ref, mobility_ref, trans_ref, mask_ref, cell_ref, columns_ref, yn_ref, yp_ref,
    fore_ref, back_ref, terms_ref, scratch_ref,
):
    row = row_index()
    middle = (row == 3) | (row == 4)
    outs = (fore_ref, lambda d: 4 - d), (back_ref, lambda d: d - 1)
    for place in range(XO):
        own = Own(place, block_ref, mobility_ref, mask_ref)
        right = [right_ref[c, place] for c in range(3)]
        cells = cell_code(place, mask_ref, cell_ref)
        kappa, source = own.kappa(), own.scale * (right[0] + right[1] + right[2])
        for out_ref, at in outs:
            distance = next(d for d in range(1, 5) if at(d) == place)
            put(out_ref, distance - 1, cells)
            if distance < 4:
                for k in range(8):
                    value = trans_ref[k, place] if k < 6 else (kappa if k == 6 else source)
                    put(out_ref, X_FIELD + 3 * k + distance - 1, value)
            if distance == 1:
                vem = [own.mask * v for v in own.solve(right)] + own.of_pressure() + own.of_flux()
                for f in range(9):
                    put(out_ref, X_VEM + f, vem[f])
    for out_ref, at in outs:
        for k in range(8):
            near, far = [y_halo(yn_ref, yp_ref, Y_FIELD + 2 * k, at(d)) for d in (1, 2)]
            put(out_ref, X_CORNER + k, jnp.where(middle, turned(far, 4), near))
        near, mid, far = [y_halo(yn_ref, yp_ref, 0, at(d)) for d in (1, 2, 3)]
        put(out_ref, X_CELL13, jnp.where(middle, turned(far, 4), near))
        put(out_ref, X_CELL2, mid)
    sums = coarse_sums(cell_ref, lambda i: right_ref[0, i] + right_ref[1, i] + right_ref[2, i])
    terms = coarse_terms(sums, columns_ref, scratch_ref, group)
    terms_ref[...] = terms
    for out_ref, _ in outs:
        out_ref[8 * X_COARSE :, :128] = terms
        out_ref[8 * X_COARSE :, 128:] = jnp.zeros((16, 128), F32)


def write_slots(group, slots_ref, three):
    lane = lax.broadcasted_iota(jnp.int32, (1, 128), 1)
    zero = jnp.zeros((1, 128), F32)
    for b in range(group):
        slots_ref[b, 6:8, :] = jnp.zeros((2, 128), F32)
        for i, line in enumerate(three):
            after = line(b + 1) if b + 1 < group else zero
            before = line(b - 1) if b > 0 else zero
            slots_ref[b, i : i + 1, :] = line(b)
            slots_ref[b, 3 + i : 4 + i, :] = jnp.where(lane < NC, after, before)


def three_groups(terms_ref, next_ref, previous_ref, start):
    return (
        lambda b: terms_ref[b : b + 1, :],
        lambda b: next_ref[start + b : start + b + 1, :128],
        lambda b: previous_ref[start + b : start + b + 1, :128],
    )


def slots_kernel(group, terms_ref, next_ref, previous_ref, slots_ref):
    write_slots(group, slots_ref, three_groups(terms_ref, next_ref, previous_ref, 0))


def forward_kernel(group, terms_ref, source_ref, solved_ref, next_ref, previous_ref, slots_ref, up_ref, down_ref):
    write_slots(group, slots_ref, three_groups(terms_ref, next_ref, previous_ref, 8 * X2_COARSE))

    def source(place):
        if place < 4:
            return source_ref[place]
        return get(next_ref, X2_S + place - 4) if place < 8 else get(previous_ref, X2_S + 11 - place)

    for out_ref, to_next in ((up_ref, True), (down_ref, False)):
        for half in range(4):
            put(out_ref, half, paired([source(Y2_PLACES[2 * half]), source(Y2_PLACES[2 * half + 1])], to_next))
        out_ref[8 * Y2_TILES - 4 :, :] = jnp.zeros((4, 256), F32)
        edge = 7 if to_next else 0
        for f in range(3):
            for place in range(XO):
                spot = 8 * Y2_V + 4 * f + place
                out_ref[spot : spot + 1, :] = solved_ref[f, place, edge : edge + 1, :]


class Fields:
    def __init__(self, trans_ref, xn_ref, xp_ref, yn_ref, yp_ref, own):
        self.trans_ref, self.x, self.y, self.own = trans_ref, (xn_ref, xp_ref), (yn_ref, yp_ref), own

    def side(self, place):
        return (self.x[0], place - 3) if place < 8 else (self.x[1], 12 - place)

    def field(self, k, place, tile):
        if place < 4:
            if tile:
                return y_halo(self.y[0], self.y[1], Y_FIELD + 2 * k, place)
            return self.trans_ref[k, place] if k < 6 else self.own(k, place)
        ref, d = self.side(place)
        if tile == 0:
            return get(ref, X_FIELD + 3 * k + d - 1)
        corner = get(ref, X_CORNER + k)
        return corner if d == 1 else turned(corner, 4)

    def trans(self, face, place, tile):
        return self.field(face, place, tile)

    def cells(self, place, tile, own_cells):
        if place < 4:
            return y_halo(self.y[0], self.y[1], 0, place) if tile else own_cells(place)
        ref, d = self.side(place)
        if tile == 0:
            return get(ref, d - 1)
        if d == 2:
            return get(ref, X_CELL2)
        corner = get(ref, X_CELL13)
        return corner if d == 1 else turned(corner, 4)

    def vem(self, f, place, tile):
        if tile == 0:
            return get(self.x[0] if place == 4 else self.x[1], X_VEM + f)
        return edge_rows(self.y[0], self.y[1], 8 * Y_VEM + 4 * f + place)


def edge_rows(next_ref, previous_ref, spot):
    after = jnp.broadcast_to(next_ref[spot : spot + 1, :], (ROWS, 256))
    before = jnp.broadcast_to(previous_ref[spot : spot + 1, :], (ROWS, 256))
    return jnp.where(row_index() < 4, after, before)


def picked(coarse, code, tile, group):
    index = jnp.maximum(code, 0.0).astype(jnp.int32)
    if tile:
        index = index + jnp.where(row_index() < 4, 0, NC)
    line = 3 * tile + group
    table = jnp.broadcast_to(coarse[line : line + 1, :], (ROWS, 128))
    found = [jnp.take_along_axis(table, index[:, 128 * h : 128 * h + 128], axis=1) for h in range(2)]
    return jnp.where(code >= 0.0, jnp.concatenate(found, axis=1), 0.0)


def application(group, fields, slots_ref, own_cells, source, solved, owns, p_ref, q_ref, z_ref, zo_ref, w_ref):
    coarse = slots_ref[0]
    for b in range(1, group):
        coarse = coarse + slots_ref[b]
    for place in range(12):
        for tile in range(2):
            if tile and place in (7, 8):
                continue
            code = fields.cells(place, tile, own_cells)
            p_ref[2 * place + tile] = picked(coarse, code, tile, (place >= 4) + (place >= 8))

    def sweep(from_ref, to_ref, both, single):
        def pressure(place, tile):
            return from_ref[2 * place + tile]

        for place in both + single:
            tiles = (0, 1) if place in both else (0,)
            for tile, total in zip(tiles, flux(pressure, fields.trans, place, tiles), strict=True):
                to_ref[2 * place + tile] = (
                    (1.0 - DAMPING) * pressure(place, tile)
                    + source(place, tile)
                    + fields.field(6, place, tile) * total
                )

    sweep(p_ref, q_ref, (0, 1, 2, 3, 4, 5, 10, 11), (6, 9))
    sweep(q_ref, p_ref, (0, 1, 2, 3, 4, 11), (5, 10))

    def pressure(place, tile):
        return p_ref[2 * place + tile]

    for place in (0, 1, 2, 3, 4, 11):
        tiles = (0, 1) if place < 4 else (0,)
        for tile, total in zip(tiles, flux(pressure, fields.trans, place, tiles), strict=True):
            p = pressure(place, tile)
            inside = place < 4 and tile == 0
            if inside:
                own = owns(place)
                e, m = own.of_pressure(), own.of_flux()
            else:
                e, m = ([fields.vem(3 * part + c, place, tile) for c in range(3)] for part in (1, 2))
            v = solved(place, tile)
            for c in range(3):
                z = v[c] + e[c] * p + m[c] * total
                if inside:
                    zo_ref[c, place] = z
                    z = own.mask * z
                z_ref[c, 2 * place + tile] = z
    for place in range(4):
        own = owns(place)
        fluxes = [flux(lambda i, t, c=c: z_ref[c, 2 * i + t], fields.trans, place, (0,))[0] for c in range(3)]
        z = [zo_ref[c, place] for c in range(3)]
        for c in range(3):
            direct = own.block[c][0] * z[0] + own.block[c][1] * z[1] + own.block[c][2] * z[2]
            total = fluxes[0] if c == 0 else fluxes[0] + fluxes[c]
            w_ref[c, place] = own.mask * (direct - own.mobility[c] * total) + own.rest * z[c]


def first_kernel(
    group, right_ref, block_ref, mobility_ref, trans_ref, mask_ref, cell_ref, columns_ref,
    xn_ref, xp_ref, yn_ref, yp_ref, slots_ref,
    zo_ref, w_ref, fore_ref, back_ref, terms_ref, source_ref, solved_ref,
    p_ref, q_ref, z_ref, scratch_ref, kappa_ref,
):
    def owns(place):
        return Own(place, block_ref, mobility_ref, mask_ref)

    def right(place):
        return [right_ref[c, place] for c in range(3)]

    for place in range(4):
        own = owns(place)
        r = right(place)
        kappa_ref[place] = own.kappa()
        source_ref[place] = own.scale * (r[0] + r[1] + r[2])
        v = own.solve(r)
        for c in range(3):
            solved_ref[c, place] = v[c]
    fields = Fields(
        trans_ref, xn_ref, xp_ref, yn_ref, yp_ref,
        lambda k, place: kappa_ref[place] if k == 6 else source_ref[place],
    )

    def solved(place, tile):
        if place < 4 and tile == 0:
            return [solved_ref[c, place] for c in range(3)]
        return [fields.vem(c, place, tile) for c in range(3)]

    application(
        group, fields, slots_ref, lambda place: cell_code(place, mask_ref, cell_ref),
        lambda place, tile: fields.field(7, place, tile), solved, owns, p_ref, q_ref, z_ref, zo_ref, w_ref,
    )
    for place in range(4):
        own = owns(place)
        w = [w_ref[c, place] for c in range(3)]
        source = own.scale * (w[0] + w[1] + w[2])
        v = [own.mask * part for part in own.solve(w)]
        source_ref[place] = source
        for c in range(3):
            solved_ref[c, place] = v[c]
        for out_ref, distance in ((fore_ref, 4 - place), (back_ref, place + 1)):
            if distance < 4:
                put(out_ref, X2_S + distance - 1, source)
            if distance == 1:
                for c in range(3):
                    put(out_ref, c, v[c])
    sums = coarse_sums(cell_ref, lambda i: w_ref[0, i] + w_ref[1, i] + w_ref[2, i])
    terms = coarse_terms(sums, columns_ref, scratch_ref, group)
    terms_ref[...] = terms
    for out_ref in (fore_ref, back_ref):
        out_ref[8 * X2_COARSE :, :128] = terms
        out_ref[8 * X2_COARSE :, 128:] = jnp.zeros((16, 128), F32)


def second_kernel(
    group, right_ref, block_ref, mobility_ref, trans_ref, mask_ref, cell_ref,
    xn_ref, xp_ref, yn_ref, yp_ref, slots_ref, w1_ref, source_ref, xn2_ref, xp2_ref, yn2_ref, yp2_ref,
    zo_ref, sums_ref,
    w_ref, p_ref, q_ref, z_ref, kappa_ref,
):
    def owns(place):
        return Own(place, block_ref, mobility_ref, mask_ref)

    for place in range(4):
        kappa_ref[place] = owns(place).kappa()
    fields = Fields(trans_ref, xn_ref, xp_ref, yn_ref, yp_ref, lambda k, place: kappa_ref[place])

    def source(place, tile):
        if tile:
            at = Y2_PLACES.index(place)
            return halo_tile(get(yn2_ref, at // 2), get(yp2_ref, at // 2), at % 2)
        if place < 4:
            return source_ref[place]
        return get(xn2_ref, X2_S + place - 4) if place < 8 else get(xp2_ref, X2_S + 11 - place)

    def solved(place, tile):
        if tile:
            return [edge_rows(yn2_ref, yp2_ref, 8 * Y2_V + 4 * c + place) for c in range(3)]
        if place < 4:
            return owns(place).solve([w1_ref[c, place] for c in range(3)])
        return [get(xn2_ref if place == 4 else xp2_ref, c) for c in range(3)]

    application(
        group, fields, slots_ref, lambda place: cell_code(place, mask_ref, cell_ref),
        source, solved, owns, p_ref, q_ref, z_ref, zo_ref, w_ref,
    )
    lane = lax.broadcasted_iota(jnp.int32, (1, 128), 1)
    totals = [jnp.zeros((ROWS, 256), F32) for _ in range(5)]
    for place in range(4):
        for c in range(3):
            a, b, r = w1_ref[c, place], w_ref[c, place], right_ref[c, place]
            for i, term in enumerate((a * a, a * b, b * b, a * r, b * r)):
                totals[i] = totals[i] + term
    line = jnp.zeros((1, 128), F32)
    for i in range(5):
        value = jnp.sum(jnp.sum(totals[i], axis=0, keepdims=True), axis=1, keepdims=True)
        line = line + jnp.where(lane == i, jnp.broadcast_to(value, (1, 128)), 0.0)
    sums_ref[...] = jnp.broadcast_to(line[None], sums_ref.shape)


def regroup_kernel(parts_ref, sums_ref):
    line = jnp.sum(parts_ref[...], axis=0)
    sums_ref[...] = jnp.broadcast_to(line[None], sums_ref.shape)


def combine_kernel(parts_ref, z1_ref, z2_ref, out_ref):
    line = jnp.sum(parts_ref[...], axis=0)
    g11, g12, g22, h1, h2 = [line[:, i : i + 1] for i in range(5)]
    determinant = g11 * g22 - g12 * g12
    c1 = jnp.broadcast_to((g22 * h1 - g12 * h2) / determinant, (ROWS, 256))
    c2 = jnp.broadcast_to((g11 * h2 - g12 * h1) / determinant, (ROWS, 256))
    for c in range(3):
        for place in range(XO):
            out_ref[c, place] = c1 * z1_ref[c, place] + c2 * z2_ref[c, place]


def call(kernel, outs, scratch, *args, smem=0):
    vmem = pl.BlockSpec(memory_space=pltpu.VMEM)
    return pl.pallas_call(
        kernel,
        out_shape=[jax.ShapeDtypeStruct(shape, F32) for shape in outs],
        in_specs=[pl.BlockSpec(memory_space=pltpu.SMEM)] * smem + [vmem] * (len(args) - smem),
        out_specs=[vmem] * len(outs),
        scratch_shapes=[pltpu.VMEM(shape, F32) for shape in scratch],
        compiler_params=pltpu.CompilerParams(vmem_limit_bytes=40 * 2**20),
    )(*args)


def send(values, axis, step):
    count = lax.axis_size(axis)
    pairs = [(i, i + step) for i in range(count) if 0 <= i + step < count]
    return lax.ppermute(values, axis, pairs)


def on_device(
    right_side, block_matrix, mobility, trans, active_mask, cell_map, coarse_owner, coarse_rows
):
    group = lax.axis_size("gy")
    line = lax.axis_size("gx")
    local = (right_side, block_matrix, mobility, trans, active_mask, cell_map)
    field = (3, XO, ROWS, 256)
    columns, up, down = call(
        functools.partial(pack_kernel, group),
        [(group, 40, 128), (8 * Y_TILES, 256), (8 * Y_TILES, 256)],
        [(ROWS, 256)],
        coarse_owner, coarse_rows, *local,
        smem=1,
    )
    columns = lax.all_to_all(columns, "gy", 0, 0)
    y_previous, y_next = send(up, "gy", 1), send(down, "gy", -1)
    fore, back, terms = call(
        functools.partial(sides_kernel, group),
        [(8 * X_TILES, 256), (8 * X_TILES, 256), (16, 128)],
        [(16, 128)],
        *local, columns, y_next, y_previous,
    )
    x_previous, x_next = send(fore, "gx", 1), send(back, "gx", -1)
    (slots,) = call(
        functools.partial(slots_kernel, group),
        [(group, 8, 128)],
        [],
        terms, x_next[8 * X_COARSE :], x_previous[8 * X_COARSE :],
    )
    slots = lax.all_to_all(slots, "gy", 0, 0)
    halos = (x_next, x_previous, y_next, y_previous)
    work = [(24, ROWS, 256), (24, ROWS, 256), (3, 24, ROWS, 256)]
    first_z, first_w, fore, back, terms, source, solved = call(
        functools.partial(first_kernel, group),
        [field, field, (8 * X2_TILES, 256), (8 * X2_TILES, 256), (16, 128), (XO, ROWS, 256), field],
        work + [(16, 128), (XO, ROWS, 256)],
        *local, columns, *halos, slots,
    )
    x2_previous, x2_next = send(fore, "gx", 1), send(back, "gx", -1)
    slots, up, down = call(
        functools.partial(forward_kernel, group),
        [(group, 8, 128), (8 * Y2_TILES, 256), (8 * Y2_TILES, 256)],
        [],
        terms, source, solved, x2_next, x2_previous,
    )
    slots = lax.all_to_all(slots, "gy", 0, 0)
    y2_previous, y2_next = send(up, "gy", 1), send(down, "gy", -1)
    second_z, sums = call(
        functools.partial(second_kernel, group),
        [field, (line, 1, 128)],
        [field] + work + [(XO, ROWS, 256)],
        *local, *halos, slots, first_w, source, x2_next, x2_previous, y2_next, y2_previous,
    )
    sums = lax.all_to_all(sums, "gx", 0, 0)
    (sums,) = call(regroup_kernel, [(group, 1, 128)], [], sums)
    sums = lax.all_to_all(sums, "gy", 0, 0)
    return call(combine_kernel, [field], [], sums, first_z, second_z)[0]


def solution(mesh):
    in_specs = (
        P(None, "gx", "gy", None),
        P(None, None, "gx", "gy", None),
        P(None, "gx", "gy", None),
        P(None, "gx", "gy", None),
        P("gx", "gy", None),
        P("gx", "gy", None),
        P("gx", "gy"),
        P(("gx", "gy"), None),
    )
    out_specs = P(None, "gx", "gy", None)
    return jax.shard_map(
        on_device, mesh=mesh, in_specs=in_specs, out_specs=out_specs, check_vma=False
    )
```

```python
import functools

import jax
import jax.numpy as jnp
from jax import lax
from jax.experimental import pallas as pl
from jax.experimental.pallas import tpu as pltpu
from jax.sharding import PartitionSpec as P

DAMPING = 0.8
F32 = jnp.float32
XO = 4
ROWS = 8
NC = 64

X_FIELD, X_VEM, X_CORNER, X_CELL13, X_CELL2, X_COARSE, X_TILES = 4, 28, 37, 45, 46, 47, 49
Y_FIELD, Y_VEM, Y_TILES = 2, 18, 23
X2_S, X2_COARSE, X2_TILES = 3, 6, 8
Y2_V, Y2_TILES = 4, 6
Y2_PLACES = (0, 1, 2, 3, 4, 5, 10, 11)


def row_index():
    return lax.broadcasted_iota(jnp.int32, (ROWS, 256), 0)


def turned(tile, by):
    return pltpu.roll(tile, by, axis=0)


def put(ref, index, tile):
    ref[8 * index : 8 * index + 8, :] = tile


def get(ref, index):
    return ref[8 * index : 8 * index + 8, :]


class Own:
    def __init__(self, place, block_ref, mobility_ref, mask_ref):
        self.mask = mask = mask_ref[place].astype(F32)
        self.rest = rest = 1.0 - mask
        self.block = [[block_ref[c, j, place] for j in range(3)] for c in range(3)]
        self.mobility = [mobility_ref[c, place] for c in range(3)]
        e = [
            [mask * self.block[c][j] + rest if c == j else mask * self.block[c][j] for j in range(3)]
            for c in range(3)
        ]
        cof = [
            [
                e[(c + 1) % 3][(j + 1) % 3] * e[(c + 2) % 3][(j + 2) % 3]
                - e[(c + 1) % 3][(j + 2) % 3] * e[(c + 2) % 3][(j + 1) % 3]
                for j in range(3)
            ]
            for c in range(3)
        ]
        recip = 1.0 / (e[0][0] * cof[0][0] + e[0][1] * cof[0][1] + e[0][2] * cof[0][2])
        self.inverse = [[cof[j][c] * recip for j in range(3)] for c in range(3)]
        self.entry = e
        self.scale = DAMPING * mask / (mask * (self.block[0][0] + self.block[1][0] + self.block[2][0]) + rest)

    def solve(self, vector):
        i = self.inverse
        return [i[c][0] * vector[0] + i[c][1] * vector[1] + i[c][2] * vector[2] for c in range(3)]

    def kappa(self):
        return self.scale * (self.mobility[0] + self.mobility[1] + self.mobility[2])

    def of_pressure(self):
        column = self.solve([self.entry[j][0] for j in range(3)])
        return [1.0 - column[0], -column[1], -column[2]]

    def of_flux(self):
        return self.solve([self.mask * self.mobility[j] for j in range(3)])


def cell_code(place, mask_ref, cell_ref):
    return jnp.where(mask_ref[place] > 0, cell_ref[place], -1).astype(F32)


def coarse_sums(cell_ref, of_row):
    wanted = lax.broadcasted_iota(jnp.int32, (NC, 256), 0)
    total = jnp.zeros((NC, 256), F32)
    for place in range(XO):
        cells, values = cell_ref[place], of_row(place)
        for row in range(ROWS):
            here = jnp.broadcast_to(cells[row : row + 1], (NC, 256)) == wanted
            total = total + jnp.where(here, jnp.broadcast_to(values[row : row + 1], (NC, 256)), 0.0)
    return jnp.sum(total[:, :128] + total[:, 128:], axis=1, keepdims=True)


def coarse_terms(sums, columns_ref, terms_ref, group):
    lane = lax.broadcasted_iota(jnp.int32, (NC // 2, 128), 1)
    weights = jnp.where(
        lane < NC,
        jnp.broadcast_to(sums[: NC // 2], (NC // 2, 128)),
        jnp.broadcast_to(sums[NC // 2 :], (NC // 2, 128)),
    )
    result = jnp.zeros(terms_ref.shape, F32)
    for j in range(group):
        terms_ref[j : j + 1, :] = columns_ref[j, NC // 2 : NC // 2 + 1, :]
    owners = terms_ref[...]
    for j in range(group):
        line = jnp.sum(columns_ref[j, : NC // 2, :] * weights, axis=0, keepdims=True)
        line = line + pltpu.roll(line, NC, axis=1)
        result = result + jnp.where(owners == float(j), jnp.broadcast_to(line, result.shape), 0.0)
    return result


def shifted_lanes(tile):
    lane = lax.broadcasted_iota(jnp.int32, (ROWS, 256), 1)
    after = jnp.where(lane < 255, pltpu.roll(tile, 255, axis=1), 0.0)
    before = jnp.where(lane > 0, pltpu.roll(tile, 1, axis=1), 0.0)
    return after, before


def flux(field, trans, place, tiles):
    own, halo = field(place, 0), field(place, 1)
    inner = row_index() < 7
    outer = row_index() > 0
    own_up, halo_up, own_down, halo_down = turned(own, 7), turned(halo, 7), turned(own, 1), turned(halo, 1)
    result = []
    for tile in tiles:
        if tile == 0:
            up, down = jnp.where(inner, own_up, halo_up), jnp.where(outer, own_down, halo_down)
        else:
            up, down = jnp.where(inner, halo_up, own_up), jnp.where(outer, halo_down, own_down)
        after, before = shifted_lanes(halo if tile else own)
        total = trans(0, place, tile) * field((place + 1) % 12, tile)
        total = total + trans(1, place, tile) * field((place + 11) % 12, tile)
        total = total + trans(2, place, tile) * up
        total = total + trans(3, place, tile) * down
        total = total + trans(4, place, tile) * after
        total = total + trans(5, place, tile) * before
        result.append(total)
    return result


def paired(tiles, to_next):
    first, second = tiles
    low = row_index() < 4
    if to_next:
        return jnp.where(low, turned(first, 4), second)
    return jnp.where(low, first, turned(second, 4))


def halo_tile(next_pair, previous_pair, which):
    low = row_index() < 4
    if which == 0:
        return jnp.where(low, next_pair, turned(previous_pair, 4))
    return jnp.where(low, turned(next_pair, 4), previous_pair)


def pack_kernel(
    group, owner_ref, rows_hbm, right_hbm, block_hbm, mobility_hbm, trans_hbm, mask_hbm, cell_hbm,
    columns_ref, up_ref, down_ref,
    field_ref, rows_ref, right_ref, block_ref, mobility_ref, trans_ref, mask_ref, cell_ref, sems,
):
    pairs = (
        (rows_hbm, rows_ref), (block_hbm, block_ref), (right_hbm, right_ref), (mobility_hbm, mobility_ref),
        (trans_hbm, trans_ref), (mask_hbm, mask_ref), (cell_hbm, cell_ref),
    )
    copies = [pltpu.make_async_copy(a, b, sems.at[i]) for i, (a, b) in enumerate(pairs)]
    for copy in copies:
        copy.start()
    copies[0].wait()
    lane = lax.broadcasted_iota(jnp.int32, (NC // 2, 128), 1)
    owner = jnp.full((8, 128), owner_ref[0, 0], jnp.int32).astype(F32)
    for pair in range(group // 2):
        part = rows_ref[:, 128 * pair : 128 * pair + 128]
        flipped = jnp.concatenate([part, part], axis=0).T
        for odd in range(2):
            block = flipped[NC * odd : NC * odd + NC]
            columns_ref[2 * pair + odd, : NC // 2, :] = jnp.where(lane < NC, block[: NC // 2], block[NC // 2 :])
            columns_ref[2 * pair + odd, NC // 2 :, :] = owner
    for copy in copies[1:]:
        copy.wait()
    for out_ref in (up_ref, down_ref):
        out_ref[8 * Y_TILES - 4 :, :] = jnp.zeros((4, 256), F32)
    for half in range(2):
        cells, fields = [], []
        for place in (2 * half, 2 * half + 1):
            own = Own(place, block_ref, mobility_ref, mask_ref)
            cells.append(cell_code(place, mask_ref, cell_ref))
            right = [right_ref[c, place] for c in range(3)]
            fields.append(
                [trans_ref[face, place] for face in range(6)]
                + [own.kappa(), own.scale * (right[0] + right[1] + right[2])]
            )
            vem = [own.mask * v for v in own.solve(right)] + own.of_pressure() + own.of_flux()
            for f in range(9):
                field_ref[...] = vem[f]
                spot = 8 * Y_VEM + 4 * f + place
                up_ref[spot : spot + 1, :] = field_ref[7:8, :]
                down_ref[spot : spot + 1, :] = field_ref[0:1, :]
        for out_ref, to_next in ((up_ref, True), (down_ref, False)):
            put(out_ref, half, paired(cells, to_next))
            for k in range(8):
                put(out_ref, Y_FIELD + 2 * k + half, paired([fields[0][k], fields[1][k]], to_next))


def y_halo(next_ref, previous_ref, index, place):
    at = index + place // 2
    return halo_tile(get(next_ref, at), get(previous_ref, at), place % 2)


def sides_kernel(
    group, right_ref, block_ref, mobility_ref, trans_ref, mask_ref, cell_ref, columns_ref, yn_ref, yp_ref,
    fore_ref, back_ref, terms_ref, scratch_ref,
):
    row = row_index()
    middle = (row == 3) | (row == 4)
    outs = (fore_ref, lambda d: 4 - d), (back_ref, lambda d: d - 1)
    for place in range(XO):
        own = Own(place, block_ref, mobility_ref, mask_ref)
        right = [right_ref[c, place] for c in range(3)]
        cells = cell_code(place, mask_ref, cell_ref)
        kappa, source = own.kappa(), own.scale * (right[0] + right[1] + right[2])
        for out_ref, at in outs:
            distance = next(d for d in range(1, 5) if at(d) == place)
            put(out_ref, distance - 1, cells)
            if distance < 4:
                for k in range(8):
                    value = trans_ref[k, place] if k < 6 else (kappa if k == 6 else source)
                    put(out_ref, X_FIELD + 3 * k + distance - 1, value)
            if distance == 1:
                vem = [own.mask * v for v in own.solve(right)] + own.of_pressure() + own.of_flux()
                for f in range(9):
                    put(out_ref, X_VEM + f, vem[f])
    for out_ref, at in outs:
        for k in range(8):
            near, far = [y_halo(yn_ref, yp_ref, Y_FIELD + 2 * k, at(d)) for d in (1, 2)]
            put(out_ref, X_CORNER + k, jnp.where(middle, turned(far, 4), near))
        near, mid, far = [y_halo(yn_ref, yp_ref, 0, at(d)) for d in (1, 2, 3)]
        put(out_ref, X_CELL13, jnp.where(middle, turned(far, 4), near))
        put(out_ref, X_CELL2, mid)
    sums = coarse_sums(cell_ref, lambda i: right_ref[0, i] + right_ref[1, i] + right_ref[2, i])
    terms = coarse_terms(sums, columns_ref, scratch_ref, group)
    terms_ref[...] = terms
    for out_ref, _ in outs:
        out_ref[8 * X_COARSE :, :128] = terms
        out_ref[8 * X_COARSE :, 128:] = jnp.zeros((16, 128), F32)


def write_slots(group, slots_ref, three):
    lane = lax.broadcasted_iota(jnp.int32, (1, 128), 1)
    zero = jnp.zeros((1, 128), F32)
    for b in range(group):
        slots_ref[b, 6:8, :] = jnp.zeros((2, 128), F32)
        for i, line in enumerate(three):
            after = line(b + 1) if b + 1 < group else zero
            before = line(b - 1) if b > 0 else zero
            slots_ref[b, i : i + 1, :] = line(b)
            slots_ref[b, 3 + i : 4 + i, :] = jnp.where(lane < NC, after, before)


def three_groups(terms_ref, next_ref, previous_ref, start):
    return (
        lambda b: terms_ref[b : b + 1, :],
        lambda b: next_ref[start + b : start + b + 1, :128],
        lambda b: previous_ref[start + b : start + b + 1, :128],
    )


def slots_kernel(group, terms_ref, next_ref, previous_ref, slots_ref):
    write_slots(group, slots_ref, three_groups(terms_ref, next_ref, previous_ref, 0))


def forward_kernel(group, terms_ref, source_ref, solved_ref, next_ref, previous_ref, slots_ref, up_ref, down_ref):
    write_slots(group, slots_ref, three_groups(terms_ref, next_ref, previous_ref, 8 * X2_COARSE))

    def source(place):
        if place < 4:
            return source_ref[place]
        return get(next_ref, X2_S + place - 4) if place < 8 else get(previous_ref, X2_S + 11 - place)

    for out_ref, to_next in ((up_ref, True), (down_ref, False)):
        for half in range(4):
            put(out_ref, half, paired([source(Y2_PLACES[2 * half]), source(Y2_PLACES[2 * half + 1])], to_next))
        out_ref[8 * Y2_TILES - 4 :, :] = jnp.zeros((4, 256), F32)
        edge = 7 if to_next else 0
        for f in range(3):
            for place in range(XO):
                spot = 8 * Y2_V + 4 * f + place
                out_ref[spot : spot + 1, :] = solved_ref[f, place, edge : edge + 1, :]


class Fields:
    def __init__(self, trans_ref, xn_ref, xp_ref, yn_ref, yp_ref, own):
        self.trans_ref, self.x, self.y, self.own = trans_ref, (xn_ref, xp_ref), (yn_ref, yp_ref), own

    def side(self, place):
        return (self.x[0], place - 3) if place < 8 else (self.x[1], 12 - place)

    def field(self, k, place, tile):
        if place < 4:
            if tile:
                return y_halo(self.y[0], self.y[1], Y_FIELD + 2 * k, place)
            return self.trans_ref[k, place] if k < 6 else self.own(k, place)
        ref, d = self.side(place)
        if tile == 0:
            return get(ref, X_FIELD + 3 * k + d - 1)
        corner = get(ref, X_CORNER + k)
        return corner if d == 1 else turned(corner, 4)

    def trans(self, face, place, tile):
        return self.field(face, place, tile)

    def cells(self, place, tile, own_cells):
        if place < 4:
            return y_halo(self.y[0], self.y[1], 0, place) if tile else own_cells(place)
        ref, d = self.side(place)
        if tile == 0:
            return get(ref, d - 1)
        if d == 2:
            return get(ref, X_CELL2)
        corner = get(ref, X_CELL13)
        return corner if d == 1 else turned(corner, 4)

    def vem(self, f, place, tile):
        if tile == 0:
            return get(self.x[0] if place == 4 else self.x[1], X_VEM + f)
        return edge_rows(self.y[0], self.y[1], 8 * Y_VEM + 4 * f + place)


def edge_rows(next_ref, previous_ref, spot):
    after = jnp.broadcast_to(next_ref[spot : spot + 1, :], (ROWS, 256))
    before = jnp.broadcast_to(previous_ref[spot : spot + 1, :], (ROWS, 256))
    return jnp.where(row_index() < 4, after, before)


def picked(coarse, code, tile, group):
    index = jnp.maximum(code, 0.0).astype(jnp.int32)
    if tile:
        index = index + jnp.where(row_index() < 4, 0, NC)
    line = 3 * tile + group
    table = jnp.broadcast_to(coarse[line : line + 1, :], (ROWS, 128))
    found = [jnp.take_along_axis(table, index[:, 128 * h : 128 * h + 128], axis=1) for h in range(2)]
    return jnp.where(code >= 0.0, jnp.concatenate(found, axis=1), 0.0)


def application(group, fields, slots_ref, own_cells, source, solved, owns, p_ref, q_ref, z_ref, zo_ref, w_ref):
    coarse = slots_ref[0]
    for b in range(1, group):
        coarse = coarse + slots_ref[b]
    for place in range(12):
        for tile in range(2):
            if tile and place in (7, 8):
                continue
            code = fields.cells(place, tile, own_cells)
            p_ref[2 * place + tile] = picked(coarse, code, tile, (place >= 4) + (place >= 8))

    def sweep(from_ref, to_ref, both, single):
        def pressure(place, tile):
            return from_ref[2 * place + tile]

        for place in both + single:
            tiles = (0, 1) if place in both else (0,)
            for tile, total in zip(tiles, flux(pressure, fields.trans, place, tiles), strict=True):
                to_ref[2 * place + tile] = (
                    (1.0 - DAMPING) * pressure(place, tile)
                    + source(place, tile)
                    + fields.field(6, place, tile) * total
                )

    sweep(p_ref, q_ref, (0, 1, 2, 3, 4, 5, 10, 11), (6, 9))
    sweep(q_ref, p_ref, (0, 1, 2, 3, 4, 11), (5, 10))

    def pressure(place, tile):
        return p_ref[2 * place + tile]

    for place in (0, 1, 2, 3, 4, 11):
        tiles = (0, 1) if place < 4 else (0,)
        for tile, total in zip(tiles, flux(pressure, fields.trans, place, tiles), strict=True):
            p = pressure(place, tile)
            inside = place < 4 and tile == 0
            if inside:
                own = owns(place)
                e, m = own.of_pressure(), own.of_flux()
            else:
                e, m = ([fields.vem(3 * part + c, place, tile) for c in range(3)] for part in (1, 2))
            v = solved(place, tile)
            for c in range(3):
                z = v[c] + e[c] * p + m[c] * total
                if inside:
                    zo_ref[c, place] = z
                    z = own.mask * z
                z_ref[c, 2 * place + tile] = z
    for place in range(4):
        own = owns(place)
        fluxes = [flux(lambda i, t, c=c: z_ref[c, 2 * i + t], fields.trans, place, (0,))[0] for c in range(3)]
        z = [zo_ref[c, place] for c in range(3)]
        for c in range(3):
            direct = own.block[c][0] * z[0] + own.block[c][1] * z[1] + own.block[c][2] * z[2]
            total = fluxes[0] if c == 0 else fluxes[0] + fluxes[c]
            w_ref[c, place] = own.mask * (direct - own.mobility[c] * total) + own.rest * z[c]


def first_kernel(
    group, right_ref, block_ref, mobility_ref, trans_ref, mask_ref, cell_ref, columns_ref,
    xn_ref, xp_ref, yn_ref, yp_ref, slots_ref,
    zo_ref, w_ref, fore_ref, back_ref, terms_ref, source_ref, solved_ref,
    p_ref, q_ref, z_ref, scratch_ref, kappa_ref,
):
    def owns(place):
        return Own(place, block_ref, mobility_ref, mask_ref)

    def right(place):
        return [right_ref[c, place] for c in range(3)]

    for place in range(4):
        own = owns(place)
        r = right(place)
        kappa_ref[place] = own.kappa()
        source_ref[place] = own.scale * (r[0] + r[1] + r[2])
        v = own.solve(r)
        for c in range(3):
            solved_ref[c, place] = v[c]
    fields = Fields(
        trans_ref, xn_ref, xp_ref, yn_ref, yp_ref,
        lambda k, place: kappa_ref[place] if k == 6 else source_ref[place],
    )

    def solved(place, tile):
        if place < 4 and tile == 0:
            return [solved_ref[c, place] for c in range(3)]
        return [fields.vem(c, place, tile) for c in range(3)]

    application(
        group, fields, slots_ref, lambda place: cell_code(place, mask_ref, cell_ref),
        lambda place, tile: fields.field(7, place, tile), solved, owns, p_ref, q_ref, z_ref, zo_ref, w_ref,
    )
    for place in range(4):
        own = owns(place)
        w = [w_ref[c, place] for c in range(3)]
        source = own.scale * (w[0] + w[1] + w[2])
        v = [own.mask * part for part in own.solve(w)]
        source_ref[place] = source
        for c in range(3):
            solved_ref[c, place] = v[c]
        for out_ref, distance in ((fore_ref, 4 - place), (back_ref, place + 1)):
            if distance < 4:
                put(out_ref, X2_S + distance - 1, source)
            if distance == 1:
                for c in range(3):
                    put(out_ref, c, v[c])
    sums = coarse_sums(cell_ref, lambda i: w_ref[0, i] + w_ref[1, i] + w_ref[2, i])
    terms = coarse_terms(sums, columns_ref, scratch_ref, group)
    terms_ref[...] = terms
    for out_ref in (fore_ref, back_ref):
        out_ref[8 * X2_COARSE :, :128] = terms
        out_ref[8 * X2_COARSE :, 128:] = jnp.zeros((16, 128), F32)


def second_kernel(
    group, right_ref, block_ref, mobility_ref, trans_ref, mask_ref, cell_ref,
    xn_ref, xp_ref, yn_ref, yp_ref, slots_ref, w1_ref, source_ref, xn2_ref, xp2_ref, yn2_ref, yp2_ref,
    zo_ref, sums_ref,
    w_ref, p_ref, q_ref, z_ref, kappa_ref,
):
    def owns(place):
        return Own(place, block_ref, mobility_ref, mask_ref)

    for place in range(4):
        kappa_ref[place] = owns(place).kappa()
    fields = Fields(trans_ref, xn_ref, xp_ref, yn_ref, yp_ref, lambda k, place: kappa_ref[place])

    def source(place, tile):
        if tile:
            at = Y2_PLACES.index(place)
            return halo_tile(get(yn2_ref, at // 2), get(yp2_ref, at // 2), at % 2)
        if place < 4:
            return source_ref[place]
        return get(xn2_ref, X2_S + place - 4) if place < 8 else get(xp2_ref, X2_S + 11 - place)

    def solved(place, tile):
        if tile:
            return [edge_rows(yn2_ref, yp2_ref, 8 * Y2_V + 4 * c + place) for c in range(3)]
        if place < 4:
            return owns(place).solve([w1_ref[c, place] for c in range(3)])
        return [get(xn2_ref if place == 4 else xp2_ref, c) for c in range(3)]

    application(
        group, fields, slots_ref, lambda place: cell_code(place, mask_ref, cell_ref),
        source, solved, owns, p_ref, q_ref, z_ref, zo_ref, w_ref,
    )
    lane = lax.broadcasted_iota(jnp.int32, (1, 128), 1)
    totals = [jnp.zeros((ROWS, 256), F32) for _ in range(5)]
    for place in range(4):
        for c in range(3):
            a, b, r = w1_ref[c, place], w_ref[c, place], right_ref[c, place]
            for i, term in enumerate((a * a, a * b, b * b, a * r, b * r)):
                totals[i] = totals[i] + term
    line = jnp.zeros((1, 128), F32)
    for i in range(5):
        value = jnp.sum(jnp.sum(totals[i], axis=0, keepdims=True), axis=1, keepdims=True)
        line = line + jnp.where(lane == i, jnp.broadcast_to(value, (1, 128)), 0.0)
    sums_ref[...] = jnp.broadcast_to(line[None], sums_ref.shape)


def regroup_kernel(parts_ref, sums_ref):
    line = jnp.sum(parts_ref[...], axis=0)
    sums_ref[...] = jnp.broadcast_to(line[None], sums_ref.shape)


def combine_kernel(parts_ref, z1_ref, z2_ref, out_ref):
    line = jnp.sum(parts_ref[...], axis=0)
    g11, g12, g22, h1, h2 = [line[:, i : i + 1] for i in range(5)]
    determinant = g11 * g22 - g12 * g12
    c1 = jnp.broadcast_to((g22 * h1 - g12 * h2) / determinant, (ROWS, 256))
    c2 = jnp.broadcast_to((g11 * h2 - g12 * h1) / determinant, (ROWS, 256))
    for c in range(3):
        for place in range(XO):
            out_ref[c, place] = c1 * z1_ref[c, place] + c2 * z2_ref[c, place]


def call(kernel, outs, scratch, *args, smem=0, space=pltpu.VMEM):
    vmem = pl.BlockSpec(memory_space=pltpu.VMEM)
    return pl.pallas_call(
        kernel,
        out_shape=[jax.ShapeDtypeStruct(shape, F32) for shape in outs],
        in_specs=[pl.BlockSpec(memory_space=pltpu.SMEM)] * smem + [pl.BlockSpec(memory_space=space)] * (len(args) - smem),
        out_specs=[vmem] * len(outs),
        scratch_shapes=[pltpu.VMEM(shape, F32) if isinstance(shape, tuple) else shape for shape in scratch],
        compiler_params=pltpu.CompilerParams(vmem_limit_bytes=40 * 2**20),
    )(*args)


def send(values, axis, step):
    count = lax.axis_size(axis)
    pairs = [(i, i + step) for i in range(count) if 0 <= i + step < count]
    return lax.ppermute(values, axis, pairs)


def on_device(
    right_side, block_matrix, mobility, trans, active_mask, cell_map, coarse_owner, coarse_rows
):
    group = lax.axis_size("gy")
    line = lax.axis_size("gx")
    local = (right_side, block_matrix, mobility, trans, active_mask, cell_map)
    field = (3, XO, ROWS, 256)
    columns, up, down = call(
        functools.partial(pack_kernel, group),
        [(group, 40, 128), (8 * Y_TILES, 256), (8 * Y_TILES, 256)],
        [(ROWS, 256), coarse_rows.shape]
        + [pltpu.VMEM(arg.shape, arg.dtype) for arg in local]
        + [pltpu.SemaphoreType.DMA((7,))],
        coarse_owner, *[pltpu.with_memory_space_constraint(arg, pltpu.HBM) for arg in (coarse_rows, *local)],
        smem=1, space=pltpu.HBM,
    )
    columns = lax.all_to_all(columns, "gy", 0, 0)
    y_previous, y_next = send(up, "gy", 1), send(down, "gy", -1)
    fore, back, terms = call(
        functools.partial(sides_kernel, group),
        [(8 * X_TILES, 256), (8 * X_TILES, 256), (16, 128)],
        [(16, 128)],
        *local, columns, y_next, y_previous,
    )
    x_previous, x_next = send(fore, "gx", 1), send(back, "gx", -1)
    (slots,) = call(
        functools.partial(slots_kernel, group),
        [(group, 8, 128)],
        [],
        terms, x_next[8 * X_COARSE :], x_previous[8 * X_COARSE :],
    )
    slots = lax.all_to_all(slots, "gy", 0, 0)
    halos = (x_next, x_previous, y_next, y_previous)
    work = [(24, ROWS, 256), (24, ROWS, 256), (3, 24, ROWS, 256)]
    first_z, first_w, fore, back, terms, source, solved = call(
        functools.partial(first_kernel, group),
        [field, field, (8 * X2_TILES, 256), (8 * X2_TILES, 256), (16, 128), (XO, ROWS, 256), field],
        work + [(16, 128), (XO, ROWS, 256)],
        *local, columns, *halos, slots,
    )
    x2_previous, x2_next = send(fore, "gx", 1), send(back, "gx", -1)
    slots, up, down = call(
        functools.partial(forward_kernel, group),
        [(group, 8, 128), (8 * Y2_TILES, 256), (8 * Y2_TILES, 256)],
        [],
        terms, source, solved, x2_next, x2_previous,
    )
    slots = lax.all_to_all(slots, "gy", 0, 0)
    y2_previous, y2_next = send(up, "gy", 1), send(down, "gy", -1)
    second_z, sums = call(
        functools.partial(second_kernel, group),
        [field, (line, 1, 128)],
        [field] + work + [(XO, ROWS, 256)],
        *local, *halos, slots, first_w, source, x2_next, x2_previous, y2_next, y2_previous,
    )
    sums = lax.all_to_all(sums, "gx", 0, 0)
    (sums,) = call(regroup_kernel, [(group, 1, 128)], [], sums)
    sums = lax.all_to_all(sums, "gy", 0, 0)
    return call(combine_kernel, [field], [], sums, first_z, second_z)[0]


def solution(mesh):
    in_specs = (
        P(None, "gx", "gy", None),
        P(None, None, "gx", "gy", None),
        P(None, "gx", "gy", None),
        P(None, "gx", "gy", None),
        P("gx", "gy", None),
        P("gx", "gy", None),
        P("gx", "gy"),
        P(("gx", "gy"), None),
    )
    out_specs = P(None, "gx", "gy", None)
    return jax.shard_map(
        on_device, mesh=mesh, in_specs=in_specs, out_specs=out_specs, check_vma=False
    )
```

```python
import functools

import jax
import jax.numpy as jnp
from jax import lax
from jax.experimental import pallas as pl
from jax.experimental.pallas import tpu as pltpu
from jax.sharding import PartitionSpec as P

DAMPING = 0.8
F32 = jnp.float32
XO = 4
ROWS = 8
NC = 64

X_FIELD, X_VEM, X_TILES = 4, 28, 37
C_CELL13, C_CELL2, C_COARSE, C_TILES = 8, 9, 10, 12
Y_FIELD, Y_LAST, Y_TILES = 2, 18, 19
X2_S, X2_COARSE, X2_TILES = 3, 6, 8
Y2_V, Y2_TILES = 4, 6
Y2_PLACES = (0, 1, 2, 3, 4, 5, 10, 11)


def row_index():
    return lax.broadcasted_iota(jnp.int32, (ROWS, 256), 0)


def turned(tile, by):
    return pltpu.roll(tile, by, axis=0)


def put(ref, index, tile):
    ref[8 * index : 8 * index + 8, :] = tile


def get(ref, index):
    return ref[8 * index : 8 * index + 8, :]


class Own:
    def __init__(self, place, block_ref, mobility_ref, mask_ref):
        self.mask = mask = mask_ref[place].astype(F32)
        self.rest = rest = 1.0 - mask
        self.block = [[block_ref[c, j, place] for j in range(3)] for c in range(3)]
        self.mobility = [mobility_ref[c, place] for c in range(3)]
        e = [
            [mask * self.block[c][j] + rest if c == j else mask * self.block[c][j] for j in range(3)]
            for c in range(3)
        ]
        cof = [
            [
                e[(c + 1) % 3][(j + 1) % 3] * e[(c + 2) % 3][(j + 2) % 3]
                - e[(c + 1) % 3][(j + 2) % 3] * e[(c + 2) % 3][(j + 1) % 3]
                for j in range(3)
            ]
            for c in range(3)
        ]
        recip = 1.0 / (e[0][0] * cof[0][0] + e[0][1] * cof[0][1] + e[0][2] * cof[0][2])
        self.inverse = [[cof[j][c] * recip for j in range(3)] for c in range(3)]
        self.entry = e
        self.scale = DAMPING * mask / (mask * (self.block[0][0] + self.block[1][0] + self.block[2][0]) + rest)

    def solve(self, vector):
        i = self.inverse
        return [i[c][0] * vector[0] + i[c][1] * vector[1] + i[c][2] * vector[2] for c in range(3)]

    def kappa(self):
        return self.scale * (self.mobility[0] + self.mobility[1] + self.mobility[2])

    def of_pressure(self):
        column = self.solve([self.entry[j][0] for j in range(3)])
        return [1.0 - column[0], -column[1], -column[2]]

    def of_flux(self):
        return self.solve([self.mask * self.mobility[j] for j in range(3)])


def cell_code(place, mask_ref, cell_ref):
    return jnp.where(mask_ref[place] > 0, cell_ref[place], -1).astype(F32)


def coarse_sums(cell_ref, of_row):
    wanted = lax.broadcasted_iota(jnp.int32, (NC, 256), 0)
    total = jnp.zeros((NC, 256), F32)
    for place in range(XO):
        cells, values = cell_ref[place], of_row(place)
        for row in range(ROWS):
            here = jnp.broadcast_to(cells[row : row + 1], (NC, 256)) == wanted
            total = total + jnp.where(here, jnp.broadcast_to(values[row : row + 1], (NC, 256)), 0.0)
    return jnp.sum(total[:, :128] + total[:, 128:], axis=1, keepdims=True)


def coarse_terms(sums, columns_ref, terms_ref, group):
    lane = lax.broadcasted_iota(jnp.int32, (NC // 2, 128), 1)
    weights = jnp.where(
        lane < NC,
        jnp.broadcast_to(sums[: NC // 2], (NC // 2, 128)),
        jnp.broadcast_to(sums[NC // 2 :], (NC // 2, 128)),
    )
    result = jnp.zeros(terms_ref.shape, F32)
    for j in range(group):
        terms_ref[j : j + 1, :] = columns_ref[j, NC // 2 : NC // 2 + 1, :]
    owners = terms_ref[...]
    for j in range(group):
        line = jnp.sum(columns_ref[j, : NC // 2, :] * weights, axis=0, keepdims=True)
        line = line + pltpu.roll(line, NC, axis=1)
        result = result + jnp.where(owners == float(j), jnp.broadcast_to(line, result.shape), 0.0)
    return result


def shifted_lanes(tile):
    lane = lax.broadcasted_iota(jnp.int32, (ROWS, 256), 1)
    after = jnp.where(lane < 255, pltpu.roll(tile, 255, axis=1), 0.0)
    before = jnp.where(lane > 0, pltpu.roll(tile, 1, axis=1), 0.0)
    return after, before


def flux(field, trans, place, tiles):
    own, halo = field(place, 0), field(place, 1)
    inner = row_index() < 7
    outer = row_index() > 0
    own_up, halo_up, own_down, halo_down = turned(own, 7), turned(halo, 7), turned(own, 1), turned(halo, 1)
    result = []
    for tile in tiles:
        if tile == 0:
            up, down = jnp.where(inner, own_up, halo_up), jnp.where(outer, own_down, halo_down)
        else:
            up, down = jnp.where(inner, halo_up, own_up), jnp.where(outer, halo_down, own_down)
        after, before = shifted_lanes(halo if tile else own)
        total = trans(0, place, tile) * field((place + 1) % 12, tile)
        total = total + trans(1, place, tile) * field((place + 11) % 12, tile)
        total = total + trans(2, place, tile) * up
        total = total + trans(3, place, tile) * down
        total = total + trans(4, place, tile) * after
        total = total + trans(5, place, tile) * before
        result.append(total)
    return result


def paired(tiles, to_next):
    first, second = tiles
    low = row_index() < 4
    if to_next:
        return jnp.where(low, turned(first, 4), second)
    return jnp.where(low, first, turned(second, 4))


def halo_tile(next_pair, previous_pair, which):
    low = row_index() < 4
    if which == 0:
        return jnp.where(low, next_pair, turned(previous_pair, 4))
    return jnp.where(low, turned(next_pair, 4), previous_pair)


def pack_kernel(
    group, owner_ref, rows_hbm, right_hbm, block_hbm, mobility_hbm, trans_hbm, mask_hbm, cell_hbm,
    columns_ref, up_ref, down_ref, fore_ref, back_ref,
    field_ref, rows_ref, right_ref, block_ref, mobility_ref, trans_ref, mask_ref, cell_ref, sems,
):
    pairs = (
        (rows_hbm, rows_ref), (block_hbm, block_ref), (right_hbm, right_ref), (mobility_hbm, mobility_ref),
        (trans_hbm, trans_ref), (mask_hbm, mask_ref), (cell_hbm, cell_ref),
    )
    copies = [pltpu.make_async_copy(a, b, sems.at[i]) for i, (a, b) in enumerate(pairs)]
    for copy in copies:
        copy.start()
    copies[0].wait()
    lane = lax.broadcasted_iota(jnp.int32, (NC // 2, 128), 1)
    owner = jnp.full((8, 128), owner_ref[0, 0], jnp.int32).astype(F32)
    for pair in range(group // 2):
        part = rows_ref[:, 128 * pair : 128 * pair + 128]
        flipped = jnp.concatenate([part, part], axis=0).T
        for odd in range(2):
            block = flipped[NC * odd : NC * odd + NC]
            columns_ref[2 * pair + odd, : NC // 2, :] = jnp.where(lane < NC, block[: NC // 2], block[NC // 2 :])
            columns_ref[2 * pair + odd, NC // 2 :, :] = owner
    for copy in copies[1:]:
        copy.wait()
    for out_ref in (up_ref, down_ref):
        out_ref[8 * Y_TILES - 4 :, :] = jnp.zeros((4, 256), F32)
    for half in range(2):
        cells, fields, edges = [], [], []
        for place in (2 * half, 2 * half + 1):
            own = Own(place, block_ref, mobility_ref, mask_ref)
            cells.append(cell_code(place, mask_ref, cell_ref))
            right = [right_ref[c, place] for c in range(3)]
            fields.append(
                [trans_ref[face, place] for face in range(6)]
                + [own.kappa(), own.scale * (right[0] + right[1] + right[2])]
            )
            vem = [own.mask * v for v in own.solve(right)] + own.of_pressure() + own.of_flux()
            for out_ref, distance in ((fore_ref, 4 - place), (back_ref, place + 1)):
                put(out_ref, distance - 1, cells[-1])
                if distance < 4:
                    for k in range(8):
                        put(out_ref, X_FIELD + 3 * k + distance - 1, fields[-1][k])
                if distance == 1:
                    for f in range(9):
                        put(out_ref, X_VEM + f, vem[f])
            edges.append(vem)
        for out_ref, to_next in ((up_ref, True), (down_ref, False)):
            put(out_ref, half, paired(cells, to_next))
            free = row_index() % 4 == (0 if to_next else 3)
            for k in range(8):
                edge = [turned(edges[0][k], 1 if to_next else 3), turned(edges[1][k], 5 if to_next else 7)]
                both = jnp.where(row_index() < 4, edge[0], edge[1])
                put(out_ref, Y_FIELD + 2 * k + half, jnp.where(free, both, paired([fields[0][k], fields[1][k]], to_next)))
            for i in range(2):
                field_ref[...] = edges[i][8]
                spot = 8 * Y_LAST + 2 * half + i
                out_ref[spot : spot + 1, :] = field_ref[7:8, :] if to_next else field_ref[0:1, :]


def y_halo(next_ref, previous_ref, index, place):
    at = index + place // 2
    return halo_tile(get(next_ref, at), get(previous_ref, at), place % 2)


def sides_kernel(
    group, right_ref, cell_ref, columns_ref, yn_ref, yp_ref,
    fore_ref, back_ref, terms_ref, scratch_ref,
):
    row = row_index()
    middle = (row == 3) | (row == 4)
    sums = coarse_sums(cell_ref, lambda i: right_ref[0, i] + right_ref[1, i] + right_ref[2, i])
    terms = coarse_terms(sums, columns_ref, scratch_ref, group)
    terms_ref[...] = terms
    for out_ref, at in ((fore_ref, lambda d: 4 - d), (back_ref, lambda d: d - 1)):
        for k in range(8):
            near, far = [y_halo(yn_ref, yp_ref, Y_FIELD + 2 * k, at(d)) for d in (1, 2)]
            put(out_ref, k, jnp.where(middle, turned(far, 4), near))
        near, mid, far = [y_halo(yn_ref, yp_ref, 0, at(d)) for d in (1, 2, 3)]
        put(out_ref, C_CELL13, jnp.where(middle, turned(far, 4), near))
        put(out_ref, C_CELL2, mid)
        out_ref[8 * C_COARSE :, :128] = terms
        out_ref[8 * C_COARSE :, 128:] = jnp.zeros((16, 128), F32)


def write_slots(group, slots_ref, three):
    lane = lax.broadcasted_iota(jnp.int32, (1, 128), 1)
    zero = jnp.zeros((1, 128), F32)
    for b in range(group):
        slots_ref[b, 6:8, :] = jnp.zeros((2, 128), F32)
        for i, line in enumerate(three):
            after = line(b + 1) if b + 1 < group else zero
            before = line(b - 1) if b > 0 else zero
            slots_ref[b, i : i + 1, :] = line(b)
            slots_ref[b, 3 + i : 4 + i, :] = jnp.where(lane < NC, after, before)


def three_groups(terms_ref, next_ref, previous_ref, start):
    return (
        lambda b: terms_ref[b : b + 1, :],
        lambda b: next_ref[start + b : start + b + 1, :128],
        lambda b: previous_ref[start + b : start + b + 1, :128],
    )


def slots_kernel(group, terms_ref, next_ref, previous_ref, slots_ref):
    write_slots(group, slots_ref, three_groups(terms_ref, next_ref, previous_ref, 8 * C_COARSE))


def forward_kernel(group, terms_ref, source_ref, solved_ref, next_ref, previous_ref, slots_ref, up_ref, down_ref):
    write_slots(group, slots_ref, three_groups(terms_ref, next_ref, previous_ref, 8 * X2_COARSE))

    def source(place):
        if place < 4:
            return source_ref[place]
        return get(next_ref, X2_S + place - 4) if place < 8 else get(previous_ref, X2_S + 11 - place)

    for out_ref, to_next in ((up_ref, True), (down_ref, False)):
        for half in range(4):
            put(out_ref, half, paired([source(Y2_PLACES[2 * half]), source(Y2_PLACES[2 * half + 1])], to_next))
        out_ref[8 * Y2_TILES - 4 :, :] = jnp.zeros((4, 256), F32)
        edge = 7 if to_next else 0
        for f in range(3):
            for place in range(XO):
                spot = 8 * Y2_V + 4 * f + place
                out_ref[spot : spot + 1, :] = solved_ref[f, place, edge : edge + 1, :]


class Fields:
    def __init__(self, trans_ref, xn_ref, xp_ref, cn_ref, cp_ref, yn_ref, yp_ref, own):
        self.trans_ref, self.own = trans_ref, own
        self.x, self.corner, self.y = (xn_ref, xp_ref), (cn_ref, cp_ref), (yn_ref, yp_ref)

    def side(self, place, tile):
        refs = self.corner if tile else self.x
        return (refs[0], place - 3) if place < 8 else (refs[1], 12 - place)

    def field(self, k, place, tile):
        if place < 4:
            if tile:
                return y_halo(self.y[0], self.y[1], Y_FIELD + 2 * k, place)
            return self.trans_ref[k, place] if k < 6 else self.own(k, place)
        ref, d = self.side(place, tile)
        if tile == 0:
            return get(ref, X_FIELD + 3 * k + d - 1)
        corner = get(ref, k)
        return corner if d == 1 else turned(corner, 4)

    def trans(self, face, place, tile):
        return self.field(face, place, tile)

    def cells(self, place, tile, own_cells):
        if place < 4:
            return y_halo(self.y[0], self.y[1], 0, place) if tile else own_cells(place)
        ref, d = self.side(place, tile)
        if tile == 0:
            return get(ref, d - 1)
        if d == 2:
            return get(ref, C_CELL2)
        corner = get(ref, C_CELL13)
        return corner if d == 1 else turned(corner, 4)

    def vem(self, f, place, tile):
        if tile == 0:
            return get(self.x[0] if place == 4 else self.x[1], X_VEM + f)
        if f == 8:
            return edge_rows(self.y[0], self.y[1], 8 * Y_LAST + place, 8 * Y_LAST + place)
        spot = 8 * (Y_FIELD + 2 * f + place // 2) + 4 * (place % 2)
        return edge_rows(self.y[0], self.y[1], spot + 3, spot)


def edge_rows(next_ref, previous_ref, next_spot, previous_spot):
    after = jnp.broadcast_to(next_ref[next_spot : next_spot + 1, :], (ROWS, 256))
    before = jnp.broadcast_to(previous_ref[previous_spot : previous_spot + 1, :], (ROWS, 256))
    return jnp.where(row_index() < 4, after, before)


def picked(coarse, code, tile, group):
    index = jnp.maximum(code, 0.0).astype(jnp.int32)
    if tile:
        index = index + jnp.where(row_index() < 4, 0, NC)
    line = 3 * tile + group
    table = jnp.broadcast_to(coarse[line : line + 1, :], (ROWS, 128))
    found = [jnp.take_along_axis(table, index[:, 128 * h : 128 * h + 128], axis=1) for h in range(2)]
    return jnp.where(code >= 0.0, jnp.concatenate(found, axis=1), 0.0)


def application(group, fields, slots_ref, own_cells, source, solved, owns, p_ref, q_ref, z_ref, zo_ref, w_ref):
    coarse = slots_ref[0]
    for b in range(1, group):
        coarse = coarse + slots_ref[b]
    for place in range(12):
        for tile in range(2):
            if tile and place in (7, 8):
                continue
            code = fields.cells(place, tile, own_cells)
            p_ref[2 * place + tile] = picked(coarse, code, tile, (place >= 4) + (place >= 8))

    def sweep(from_ref, to_ref, both, single):
        def pressure(place, tile):
            return from_ref[2 * place + tile]

        for place in both + single:
            tiles = (0, 1) if place in both else (0,)
            for tile, total in zip(tiles, flux(pressure, fields.trans, place, tiles), strict=True):
                to_ref[2 * place + tile] = (
                    (1.0 - DAMPING) * pressure(place, tile)
                    + source(place, tile)
                    + fields.field(6, place, tile) * total
                )

    sweep(p_ref, q_ref, (0, 1, 2, 3, 4, 5, 10, 11), (6, 9))
    sweep(q_ref, p_ref, (0, 1, 2, 3, 4, 11), (5, 10))

    def pressure(place, tile):
        return p_ref[2 * place + tile]

    for place in (0, 1, 2, 3, 4, 11):
        tiles = (0, 1) if place < 4 else (0,)
        for tile, total in zip(tiles, flux(pressure, fields.trans, place, tiles), strict=True):
            p = pressure(place, tile)
            inside = place < 4 and tile == 0
            if inside:
                own = owns(place)
                e, m = own.of_pressure(), own.of_flux()
            else:
                e, m = ([fields.vem(3 * part + c, place, tile) for c in range(3)] for part in (1, 2))
            v = solved(place, tile)
            for c in range(3):
                z = v[c] + e[c] * p + m[c] * total
                if inside:
                    zo_ref[c, place] = z
                    z = own.mask * z
                z_ref[c, 2 * place + tile] = z
    for place in range(4):
        own = owns(place)
        fluxes = [flux(lambda i, t, c=c: z_ref[c, 2 * i + t], fields.trans, place, (0,))[0] for c in range(3)]
        z = [zo_ref[c, place] for c in range(3)]
        for c in range(3):
            direct = own.block[c][0] * z[0] + own.block[c][1] * z[1] + own.block[c][2] * z[2]
            total = fluxes[0] if c == 0 else fluxes[0] + fluxes[c]
            w_ref[c, place] = own.mask * (direct - own.mobility[c] * total) + own.rest * z[c]


def first_kernel(
    group, right_ref, block_ref, mobility_ref, trans_ref, mask_ref, cell_ref, columns_ref,
    xn_ref, xp_ref, cn_ref, cp_ref, yn_ref, yp_ref, slots_ref,
    zo_ref, w_ref, fore_ref, back_ref, terms_ref, source_ref, solved_ref,
    p_ref, q_ref, z_ref, scratch_ref, kappa_ref,
):
    def owns(place):
        return Own(place, block_ref, mobility_ref, mask_ref)

    def right(place):
        return [right_ref[c, place] for c in range(3)]

    for place in range(4):
        own = owns(place)
        r = right(place)
        kappa_ref[place] = own.kappa()
        source_ref[place] = own.scale * (r[0] + r[1] + r[2])
        v = own.solve(r)
        for c in range(3):
            solved_ref[c, place] = v[c]
    fields = Fields(
        trans_ref, xn_ref, xp_ref, cn_ref, cp_ref, yn_ref, yp_ref,
        lambda k, place: kappa_ref[place] if k == 6 else source_ref[place],
    )

    def solved(place, tile):
        if place < 4 and tile == 0:
            return [solved_ref[c, place] for c in range(3)]
        return [fields.vem(c, place, tile) for c in range(3)]

    application(
        group, fields, slots_ref, lambda place: cell_code(place, mask_ref, cell_ref),
        lambda place, tile: fields.field(7, place, tile), solved, owns, p_ref, q_ref, z_ref, zo_ref, w_ref,
    )
    for place in range(4):
        own = owns(place)
        w = [w_ref[c, place] for c in range(3)]
        source = own.scale * (w[0] + w[1] + w[2])
        v = [own.mask * part for part in own.solve(w)]
        source_ref[place] = source
        for c in range(3):
            solved_ref[c, place] = v[c]
        for out_ref, distance in ((fore_ref, 4 - place), (back_ref, place + 1)):
            if distance < 4:
                put(out_ref, X2_S + distance - 1, source)
            if distance == 1:
                for c in range(3):
                    put(out_ref, c, v[c])
    sums = coarse_sums(cell_ref, lambda i: w_ref[0, i] + w_ref[1, i] + w_ref[2, i])
    terms = coarse_terms(sums, columns_ref, scratch_ref, group)
    terms_ref[...] = terms
    for out_ref in (fore_ref, back_ref):
        out_ref[8 * X2_COARSE :, :128] = terms
        out_ref[8 * X2_COARSE :, 128:] = jnp.zeros((16, 128), F32)


def second_kernel(
    group, right_ref, block_ref, mobility_ref, trans_ref, mask_ref, cell_ref,
    xn_ref, xp_ref, cn_ref, cp_ref, yn_ref, yp_ref, slots_ref, w1_ref, source_ref, xn2_ref, xp2_ref, yn2_ref, yp2_ref,
    zo_ref, sums_ref,
    w_ref, p_ref, q_ref, z_ref, kappa_ref,
):
    def owns(place):
        return Own(place, block_ref, mobility_ref, mask_ref)

    for place in range(4):
        kappa_ref[place] = owns(place).kappa()
    fields = Fields(trans_ref, xn_ref, xp_ref, cn_ref, cp_ref, yn_ref, yp_ref, lambda k, place: kappa_ref[place])

    def source(place, tile):
        if tile:
            at = Y2_PLACES.index(place)
            return halo_tile(get(yn2_ref, at // 2), get(yp2_ref, at // 2), at % 2)
        if place < 4:
            return source_ref[place]
        return get(xn2_ref, X2_S + place - 4) if place < 8 else get(xp2_ref, X2_S + 11 - place)

    def solved(place, tile):
        if tile:
            spots = [8 * Y2_V + 4 * c + place for c in range(3)]
            return [edge_rows(yn2_ref, yp2_ref, spot, spot) for spot in spots]
        if place < 4:
            return owns(place).solve([w1_ref[c, place] for c in range(3)])
        return [get(xn2_ref if place == 4 else xp2_ref, c) for c in range(3)]

    application(
        group, fields, slots_ref, lambda place: cell_code(place, mask_ref, cell_ref),
        source, solved, owns, p_ref, q_ref, z_ref, zo_ref, w_ref,
    )
    lane = lax.broadcasted_iota(jnp.int32, (1, 128), 1)
    totals = [jnp.zeros((ROWS, 256), F32) for _ in range(5)]
    for place in range(4):
        for c in range(3):
            a, b, r = w1_ref[c, place], w_ref[c, place], right_ref[c, place]
            for i, term in enumerate((a * a, a * b, b * b, a * r, b * r)):
                totals[i] = totals[i] + term
    line = jnp.zeros((1, 128), F32)
    for i in range(5):
        value = jnp.sum(jnp.sum(totals[i], axis=0, keepdims=True), axis=1, keepdims=True)
        line = line + jnp.where(lane == i, jnp.broadcast_to(value, (1, 128)), 0.0)
    sums_ref[...] = jnp.broadcast_to(line[None], sums_ref.shape)


def regroup_kernel(parts_ref, sums_ref):
    line = jnp.sum(parts_ref[...], axis=0)
    sums_ref[...] = jnp.broadcast_to(line[None], sums_ref.shape)


def combine_kernel(parts_ref, z1_ref, z2_ref, out_ref):
    line = jnp.sum(parts_ref[...], axis=0)
    g11, g12, g22, h1, h2 = [line[:, i : i + 1] for i in range(5)]
    determinant = g11 * g22 - g12 * g12
    c1 = jnp.broadcast_to((g22 * h1 - g12 * h2) / determinant, (ROWS, 256))
    c2 = jnp.broadcast_to((g11 * h2 - g12 * h1) / determinant, (ROWS, 256))
    for c in range(3):
        for place in range(XO):
            out_ref[c, place] = c1 * z1_ref[c, place] + c2 * z2_ref[c, place]


class Sent:
    def __init__(self, axis, tiles, swap=False):
        self.axis, self.shape, self.swap = axis, (8 * tiles, 256), swap

    def exchanged(self, pair):
        count = lax.axis_size(self.axis)
        if self.swap:
            links = [[(i, i + 1) for i in range(start, count - 1, 2)] for start in (1, 0)]
            links = [way + [(j, i) for i, j in way] for way in links]
            second = lax.ppermute(pair[1], self.axis, links[1])
            first = lax.ppermute(pair[0], self.axis, links[0])
            return Received(self.axis, (first, second), True)
        from_previous = lax.ppermute(pair[0], self.axis, [(i, i + 1) for i in range(count - 1)])
        from_next = lax.ppermute(pair[1], self.axis, [(i + 1, i) for i in range(count - 1)])
        return Received(self.axis, (from_next, from_previous), False)


class Received:
    def __init__(self, axis, pair, swap):
        self.axis, self.pair, self.swap = axis, pair, swap


def copied(axis, even, odd):
    def body(pairs):
        def copy():
            for from_ref, to_ref in pairs:
                to_ref[...] = from_ref[...]

        return copy

    is_odd = lax.axis_index(axis) % 2
    pl.when(is_odd == 1)(body(odd))
    pl.when(is_odd == 0)(body(even))


def call(kernel, outs, scratch, *args, smem=0, space=pltpu.VMEM):
    vmem = pl.BlockSpec(memory_space=pltpu.VMEM)
    flat, specs, shapes, views = [], [], [], []
    for i, arg in enumerate(args):
        parts = arg.pair if isinstance(arg, Received) else [arg]
        flat += parts
        specs += [pl.BlockSpec(memory_space=pltpu.SMEM if i < smem else space)] * len(parts)
        if isinstance(arg, Received) and arg.swap:
            views += [arg.pair[0].shape] * 2
    for out in outs:
        shapes += [out.shape] * 2 if isinstance(out, Sent) else [out]
        if isinstance(out, Sent) and out.swap:
            views += [out.shape] * 2

    def body(*refs):
        refs = list(refs)
        ins, results = refs[: len(flat)], refs[len(flat) : len(flat) + len(shapes)]
        copies = refs[len(flat) + len(shapes) : len(flat) + len(shapes) + len(views)]
        rest = refs[len(flat) + len(shapes) + len(views) :]
        seen, after = [], []
        for arg in args:
            parts = [ins.pop(0) for _ in range(2 if isinstance(arg, Received) else 1)]
            if isinstance(arg, Received) and arg.swap:
                first, second = parts
                parts = ahead, behind = copies.pop(0), copies.pop(0)
                copied(arg.axis, [(second, ahead), (first, behind)], [(first, ahead), (second, behind)])
            seen += parts
        for out in outs:
            parts = [results.pop(0) for _ in range(2 if isinstance(out, Sent) else 1)]
            if isinstance(out, Sent) and out.swap:
                first, second = parts
                parts = ahead, behind = copies.pop(0), copies.pop(0)
                after.append((out.axis, [(ahead, second), (behind, first)], [(ahead, first), (behind, second)]))
            seen += parts
        kernel(*seen, *rest)
        for each in after:
            copied(*each)

    found = list(
        pl.pallas_call(
            body,
            out_shape=[jax.ShapeDtypeStruct(shape, F32) for shape in shapes],
            in_specs=specs,
            out_specs=[vmem] * len(shapes),
            scratch_shapes=[pltpu.VMEM(shape, F32) for shape in views]
            + [pltpu.VMEM(shape, F32) if isinstance(shape, tuple) else shape for shape in scratch],
            compiler_params=pltpu.CompilerParams(vmem_limit_bytes=40 * 2**20),
        )(*flat)
    )
    results = []
    for out in outs:
        if isinstance(out, Sent):
            results.append(out.exchanged([found.pop(0), found.pop(0)]))
        else:
            results.append(found.pop(0))
    return results


def on_device(
    right_side, block_matrix, mobility, trans, active_mask, cell_map, coarse_owner, coarse_rows
):
    group = lax.axis_size("gy")
    line = lax.axis_size("gx")
    local = (right_side, block_matrix, mobility, trans, active_mask, cell_map)
    field = (3, XO, ROWS, 256)
    columns, y_halos, x_halos = call(
        functools.partial(pack_kernel, group),
        [(group, 40, 128), Sent("gy", Y_TILES, True), Sent("gx", X_TILES, True)],
        [(ROWS, 256), coarse_rows.shape]
        + [pltpu.VMEM(arg.shape, arg.dtype) for arg in local]
        + [pltpu.SemaphoreType.DMA((7,))],
        coarse_owner, *[pltpu.with_memory_space_constraint(arg, pltpu.HBM) for arg in (coarse_rows, *local)],
        smem=1, space=pltpu.HBM,
    )
    columns = lax.all_to_all(columns, "gy", 0, 0)
    corners, terms = call(
        functools.partial(sides_kernel, group),
        [Sent("gx", C_TILES, True), (16, 128)],
        [(16, 128)],
        right_side, cell_map, columns, y_halos,
    )
    (slots,) = call(functools.partial(slots_kernel, group), [(group, 8, 128)], [], terms, corners)
    slots = lax.all_to_all(slots, "gy", 0, 0)
    halos = (x_halos, corners, y_halos)
    work = [(24, ROWS, 256), (24, ROWS, 256), (3, 24, ROWS, 256)]
    first_z, first_w, x2_halos, terms, source, solved = call(
        functools.partial(first_kernel, group),
        [field, field, Sent("gx", X2_TILES, True), (16, 128), (XO, ROWS, 256), field],
        work + [(16, 128), (XO, ROWS, 256)],
        *local, columns, *halos, slots,
    )
    slots, y2_halos = call(
        functools.partial(forward_kernel, group),
        [(group, 8, 128), Sent("gy", Y2_TILES, True)],
        [],
        terms, source, solved, x2_halos,
    )
    slots = lax.all_to_all(slots, "gy", 0, 0)
    second_z, sums = call(
        functools.partial(second_kernel, group),
        [field, (line, 1, 128)],
        [field] + work + [(XO, ROWS, 256)],
        *local, *halos, slots, first_w, source, x2_halos, y2_halos,
    )
    sums = lax.all_to_all(sums, "gx", 0, 0)
    (sums,) = call(regroup_kernel, [(group, 1, 128)], [], sums)
    sums = lax.all_to_all(sums, "gy", 0, 0)
    return call(combine_kernel, [field], [], sums, first_z, second_z)[0]


def solution(mesh):
    in_specs = (
        P(None, "gx", "gy", None),
        P(None, None, "gx", "gy", None),
        P(None, "gx", "gy", None),
        P(None, "gx", "gy", None),
        P("gx", "gy", None),
        P("gx", "gy", None),
        P("gx", "gy"),
        P(("gx", "gy"), None),
    )
    out_specs = P(None, "gx", "gy", None)
    return jax.shard_map(
        on_device, mesh=mesh, in_specs=in_specs, out_specs=out_specs, check_vma=False
    )
```

```python
import functools

import jax
import jax.numpy as jnp
from jax import lax
from jax.experimental import pallas as pl
from jax.experimental.pallas import tpu as pltpu
from jax.sharding import PartitionSpec as P

DAMPING = 0.8
F32 = jnp.float32
XO = 4
ROWS = 8
NC = 64

X_FIELD, X_VEM, X_TILES = 4, 28, 37
C_CELL13, C_CELL2, C_COARSE, C_TILES = 8, 9, 10, 12
Y_FIELD, Y_LAST, Y_TILES = 2, 18, 19
X2_S, X2_COARSE, X2_TILES = 3, 6, 8
Y2_V, Y2_TILES = 4, 6
Y2_PLACES = (0, 1, 2, 3, 4, 5, 10, 11)


def row_index():
    return lax.broadcasted_iota(jnp.int32, (ROWS, 256), 0)


def turned(tile, by):
    return pltpu.roll(tile, by, axis=0)


def put(ref, index, tile):
    ref[8 * index : 8 * index + 8, :] = tile


def get(ref, index):
    return ref[8 * index : 8 * index + 8, :]


class Own:
    def __init__(self, place, block_ref, mobility_ref, mask_ref):
        self.mask = mask = mask_ref[place].astype(F32)
        self.rest = rest = 1.0 - mask
        self.block = [[block_ref[c, j, place] for j in range(3)] for c in range(3)]
        self.mobility = [mobility_ref[c, place] for c in range(3)]
        e = [
            [mask * self.block[c][j] + rest if c == j else mask * self.block[c][j] for j in range(3)]
            for c in range(3)
        ]
        cof = [
            [
                e[(c + 1) % 3][(j + 1) % 3] * e[(c + 2) % 3][(j + 2) % 3]
                - e[(c + 1) % 3][(j + 2) % 3] * e[(c + 2) % 3][(j + 1) % 3]
                for j in range(3)
            ]
            for c in range(3)
        ]
        recip = 1.0 / (e[0][0] * cof[0][0] + e[0][1] * cof[0][1] + e[0][2] * cof[0][2])
        self.inverse = [[cof[j][c] * recip for j in range(3)] for c in range(3)]
        self.entry = e
        self.scale = DAMPING * mask / (mask * (self.block[0][0] + self.block[1][0] + self.block[2][0]) + rest)

    def solve(self, vector):
        i = self.inverse
        return [i[c][0] * vector[0] + i[c][1] * vector[1] + i[c][2] * vector[2] for c in range(3)]

    def kappa(self):
        return self.scale * (self.mobility[0] + self.mobility[1] + self.mobility[2])

    def of_pressure(self):
        column = self.solve([self.entry[j][0] for j in range(3)])
        return [1.0 - column[0], -column[1], -column[2]]

    def of_flux(self):
        return self.solve([self.mask * self.mobility[j] for j in range(3)])


def cell_code(place, mask_ref, cell_ref):
    return jnp.where(mask_ref[place] > 0, cell_ref[place], -1).astype(F32)


def coarse_sums(cell_ref, of_row):
    wanted = lax.broadcasted_iota(jnp.int32, (NC, 256), 0)
    total = jnp.zeros((NC, 256), F32)
    for place in range(XO):
        cells, values = cell_ref[place], of_row(place)
        for row in range(ROWS):
            here = jnp.broadcast_to(cells[row : row + 1], (NC, 256)) == wanted
            total = total + jnp.where(here, jnp.broadcast_to(values[row : row + 1], (NC, 256)), 0.0)
    return jnp.sum(total[:, :128] + total[:, 128:], axis=1, keepdims=True)


def segment(ref, j, k):
    return ref[j, :, 128 * k : 128 * k + 128]


def coarse_terms(sums, columns_ref, terms_ref, group):
    lane = lax.broadcasted_iota(jnp.int32, (NC // 2, 128), 1)
    weights = jnp.where(
        lane < NC,
        jnp.broadcast_to(sums[: NC // 2], (NC // 2, 128)),
        jnp.broadcast_to(sums[NC // 2 :], (NC // 2, 128)),
    )
    result = jnp.zeros(terms_ref.shape, F32)
    for j in range(group):
        terms_ref[j : j + 1, :] = segment(columns_ref, j, NC // 2)
    owners = terms_ref[...]
    for j in range(group):
        line = segment(columns_ref, j, 0) * weights[:1]
        for k in range(1, NC // 2):
            line = line + segment(columns_ref, j, k) * weights[k : k + 1]
        line = line + pltpu.roll(line, NC, axis=1)
        result = result + jnp.where(owners == float(j), jnp.broadcast_to(line, result.shape), 0.0)
    return result


def shifted_lanes(tile):
    lane = lax.broadcasted_iota(jnp.int32, (ROWS, 256), 1)
    after = jnp.where(lane < 255, pltpu.roll(tile, 255, axis=1), 0.0)
    before = jnp.where(lane > 0, pltpu.roll(tile, 1, axis=1), 0.0)
    return after, before


def flux(field, trans, place, tiles):
    own, halo = field(place, 0), field(place, 1)
    inner = row_index() < 7
    outer = row_index() > 0
    own_up, halo_up, own_down, halo_down = turned(own, 7), turned(halo, 7), turned(own, 1), turned(halo, 1)
    result = []
    for tile in tiles:
        if tile == 0:
            up, down = jnp.where(inner, own_up, halo_up), jnp.where(outer, own_down, halo_down)
        else:
            up, down = jnp.where(inner, halo_up, own_up), jnp.where(outer, halo_down, own_down)
        after, before = shifted_lanes(halo if tile else own)
        total = trans(0, place, tile) * field((place + 1) % 12, tile)
        total = total + trans(1, place, tile) * field((place + 11) % 12, tile)
        total = total + trans(2, place, tile) * up
        total = total + trans(3, place, tile) * down
        total = total + trans(4, place, tile) * after
        total = total + trans(5, place, tile) * before
        result.append(total)
    return result


def paired(tiles, to_next):
    first, second = tiles
    low = row_index() < 4
    if to_next:
        return jnp.where(low, turned(first, 4), second)
    return jnp.where(low, first, turned(second, 4))


def halo_tile(next_pair, previous_pair, which):
    low = row_index() < 4
    if which == 0:
        return jnp.where(low, next_pair, turned(previous_pair, 4))
    return jnp.where(low, turned(next_pair, 4), previous_pair)


def pack_kernel(
    group, owner_ref, rows_hbm, right_hbm, block_hbm, mobility_hbm, trans_hbm, mask_hbm, cell_hbm,
    columns_ref, up_ref, down_ref, fore_ref, back_ref,
    field_ref, rows_ref, right_ref, block_ref, mobility_ref, trans_ref, mask_ref, cell_ref, sems,
):
    pairs = (
        (rows_hbm, rows_ref), (block_hbm, block_ref), (right_hbm, right_ref), (mobility_hbm, mobility_ref),
        (trans_hbm, trans_ref), (mask_hbm, mask_ref), (cell_hbm, cell_ref),
    )
    copies = [pltpu.make_async_copy(a, b, sems.at[i]) for i, (a, b) in enumerate(pairs)]
    for copy in copies:
        copy.start()
    copies[0].wait()
    lane = lax.broadcasted_iota(jnp.int32, (NC // 2, 128), 1)
    owner = jnp.full((1, 128), owner_ref[0, 0], jnp.int32).astype(F32)
    for pair in range(group // 2):
        part = rows_ref[:, 128 * pair : 128 * pair + 128]
        flipped = jnp.concatenate([part, part], axis=0).T
        for odd in range(2):
            block = flipped[NC * odd : NC * odd + NC]
            block = jnp.where(lane < NC, block[: NC // 2], block[NC // 2 :])
            for k in range(NC // 2):
                columns_ref[2 * pair + odd, :, 128 * k : 128 * k + 128] = block[k : k + 1]
            columns_ref[2 * pair + odd, :, 64 * NC :] = owner
    for copy in copies[1:]:
        copy.wait()
    for out_ref in (up_ref, down_ref):
        out_ref[8 * Y_TILES - 4 :, :] = jnp.zeros((4, 256), F32)
    for half in range(2):
        cells, fields, edges = [], [], []
        for place in (2 * half, 2 * half + 1):
            own = Own(place, block_ref, mobility_ref, mask_ref)
            cells.append(cell_code(place, mask_ref, cell_ref))
            right = [right_ref[c, place] for c in range(3)]
            fields.append(
                [trans_ref[face, place] for face in range(6)]
                + [own.kappa(), own.scale * (right[0] + right[1] + right[2])]
            )
            vem = [own.mask * v for v in own.solve(right)] + own.of_pressure() + own.of_flux()
            for out_ref, distance in ((fore_ref, 4 - place), (back_ref, place + 1)):
                put(out_ref, distance - 1, cells[-1])
                if distance < 4:
                    for k in range(8):
                        put(out_ref, X_FIELD + 3 * k + distance - 1, fields[-1][k])
                if distance == 1:
                    for f in range(9):
                        put(out_ref, X_VEM + f, vem[f])
            edges.append(vem)
        for out_ref, to_next in ((up_ref, True), (down_ref, False)):
            put(out_ref, half, paired(cells, to_next))
            free = row_index() % 4 == (0 if to_next else 3)
            for k in range(8):
                edge = [turned(edges[0][k], 1 if to_next else 3), turned(edges[1][k], 5 if to_next else 7)]
                both = jnp.where(row_index() < 4, edge[0], edge[1])
                put(out_ref, Y_FIELD + 2 * k + half, jnp.where(free, both, paired([fields[0][k], fields[1][k]], to_next)))
            for i in range(2):
                field_ref[...] = edges[i][8]
                spot = 8 * Y_LAST + 2 * half + i
                out_ref[spot : spot + 1, :] = field_ref[7:8, :] if to_next else field_ref[0:1, :]


def y_halo(next_ref, previous_ref, index, place):
    at = index + place // 2
    return halo_tile(get(next_ref, at), get(previous_ref, at), place % 2)


def sides_kernel(
    group, right_ref, cell_ref, columns_ref, yn_ref, yp_ref,
    fore_ref, back_ref, terms_ref, scratch_ref,
):
    row = row_index()
    middle = (row == 3) | (row == 4)
    sums = coarse_sums(cell_ref, lambda i: right_ref[0, i] + right_ref[1, i] + right_ref[2, i])
    terms = coarse_terms(sums, columns_ref, scratch_ref, group)
    terms_ref[...] = terms
    for out_ref, at in ((fore_ref, lambda d: 4 - d), (back_ref, lambda d: d - 1)):
        for k in range(8):
            near, far = [y_halo(yn_ref, yp_ref, Y_FIELD + 2 * k, at(d)) for d in (1, 2)]
            put(out_ref, k, jnp.where(middle, turned(far, 4), near))
        near, mid, far = [y_halo(yn_ref, yp_ref, 0, at(d)) for d in (1, 2, 3)]
        put(out_ref, C_CELL13, jnp.where(middle, turned(far, 4), near))
        put(out_ref, C_CELL2, mid)
        out_ref[8 * C_COARSE :, :128] = terms
        out_ref[8 * C_COARSE :, 128:] = jnp.zeros((16, 128), F32)


def write_slots(group, slots_ref, three):
    lane = lax.broadcasted_iota(jnp.int32, (1, 128), 1)
    zero = jnp.zeros((1, 128), F32)
    for b in range(group):
        for i, line in enumerate(three):
            after = line(b + 1) if b + 1 < group else zero
            before = line(b - 1) if b > 0 else zero
            slots_ref[b, :, 128 * i : 128 * i + 128] = line(b)
            slots_ref[b, :, 128 * i + 384 : 128 * i + 512] = jnp.where(lane < NC, after, before)


def three_groups(terms_ref, next_ref, previous_ref, start):
    return (
        lambda b: terms_ref[b : b + 1, :],
        lambda b: next_ref[start + b : start + b + 1, :128],
        lambda b: previous_ref[start + b : start + b + 1, :128],
    )


def slots_kernel(group, terms_ref, next_ref, previous_ref, slots_ref):
    write_slots(group, slots_ref, three_groups(terms_ref, next_ref, previous_ref, 8 * C_COARSE))


def forward_kernel(group, terms_ref, source_ref, solved_ref, next_ref, previous_ref, slots_ref, up_ref, down_ref):
    write_slots(group, slots_ref, three_groups(terms_ref, next_ref, previous_ref, 8 * X2_COARSE))

    def source(place):
        if place < 4:
            return source_ref[place]
        return get(next_ref, X2_S + place - 4) if place < 8 else get(previous_ref, X2_S + 11 - place)

    for out_ref, to_next in ((up_ref, True), (down_ref, False)):
        for half in range(4):
            put(out_ref, half, paired([source(Y2_PLACES[2 * half]), source(Y2_PLACES[2 * half + 1])], to_next))
        out_ref[8 * Y2_TILES - 4 :, :] = jnp.zeros((4, 256), F32)
        edge = 7 if to_next else 0
        for f in range(3):
            for place in range(XO):
                spot = 8 * Y2_V + 4 * f + place
                out_ref[spot : spot + 1, :] = solved_ref[f, place, edge : edge + 1, :]


class Fields:
    def __init__(self, trans_ref, xn_ref, xp_ref, cn_ref, cp_ref, yn_ref, yp_ref, own):
        self.trans_ref, self.own = trans_ref, own
        self.x, self.corner, self.y = (xn_ref, xp_ref), (cn_ref, cp_ref), (yn_ref, yp_ref)

    def side(self, place, tile):
        refs = self.corner if tile else self.x
        return (refs[0], place - 3) if place < 8 else (refs[1], 12 - place)

    def field(self, k, place, tile):
        if place < 4:
            if tile:
                return y_halo(self.y[0], self.y[1], Y_FIELD + 2 * k, place)
            return self.trans_ref[k, place] if k < 6 else self.own(k, place)
        ref, d = self.side(place, tile)
        if tile == 0:
            return get(ref, X_FIELD + 3 * k + d - 1)
        corner = get(ref, k)
        return corner if d == 1 else turned(corner, 4)

    def trans(self, face, place, tile):
        return self.field(face, place, tile)

    def cells(self, place, tile, own_cells):
        if place < 4:
            return y_halo(self.y[0], self.y[1], 0, place) if tile else own_cells(place)
        ref, d = self.side(place, tile)
        if tile == 0:
            return get(ref, d - 1)
        if d == 2:
            return get(ref, C_CELL2)
        corner = get(ref, C_CELL13)
        return corner if d == 1 else turned(corner, 4)

    def vem(self, f, place, tile):
        if tile == 0:
            return get(self.x[0] if place == 4 else self.x[1], X_VEM + f)
        if f == 8:
            return edge_rows(self.y[0], self.y[1], 8 * Y_LAST + place, 8 * Y_LAST + place)
        spot = 8 * (Y_FIELD + 2 * f + place // 2) + 4 * (place % 2)
        return edge_rows(self.y[0], self.y[1], spot + 3, spot)


def edge_rows(next_ref, previous_ref, next_spot, previous_spot):
    after = jnp.broadcast_to(next_ref[next_spot : next_spot + 1, :], (ROWS, 256))
    before = jnp.broadcast_to(previous_ref[previous_spot : previous_spot + 1, :], (ROWS, 256))
    return jnp.where(row_index() < 4, after, before)


def picked(coarse, code, tile, group):
    index = jnp.maximum(code, 0.0).astype(jnp.int32)
    if tile:
        index = index + jnp.where(row_index() < 4, 0, NC)
    line = 3 * tile + group
    table = jnp.broadcast_to(coarse[:, 128 * line : 128 * line + 128], (ROWS, 128))
    found = [jnp.take_along_axis(table, index[:, 128 * h : 128 * h + 128], axis=1) for h in range(2)]
    return jnp.where(code >= 0.0, jnp.concatenate(found, axis=1), 0.0)


def application(group, fields, slots_ref, own_cells, source, solved, owns, p_ref, q_ref, z_ref, zo_ref, w_ref):
    coarse = slots_ref[0]
    for b in range(1, group):
        coarse = coarse + slots_ref[b]
    for place in range(12):
        for tile in range(2):
            if tile and place in (7, 8):
                continue
            code = fields.cells(place, tile, own_cells)
            p_ref[2 * place + tile] = picked(coarse, code, tile, (place >= 4) + (place >= 8))

    def sweep(from_ref, to_ref, both, single):
        def pressure(place, tile):
            return from_ref[2 * place + tile]

        for place in both + single:
            tiles = (0, 1) if place in both else (0,)
            for tile, total in zip(tiles, flux(pressure, fields.trans, place, tiles), strict=True):
                to_ref[2 * place + tile] = (
                    (1.0 - DAMPING) * pressure(place, tile)
                    + source(place, tile)
                    + fields.field(6, place, tile) * total
                )

    sweep(p_ref, q_ref, (0, 1, 2, 3, 4, 5, 10, 11), (6, 9))
    sweep(q_ref, p_ref, (0, 1, 2, 3, 4, 11), (5, 10))

    def pressure(place, tile):
        return p_ref[2 * place + tile]

    for place in (0, 1, 2, 3, 4, 11):
        tiles = (0, 1) if place < 4 else (0,)
        for tile, total in zip(tiles, flux(pressure, fields.trans, place, tiles), strict=True):
            p = pressure(place, tile)
            inside = place < 4 and tile == 0
            if inside:
                own = owns(place)
                e, m = own.of_pressure(), own.of_flux()
            else:
                e, m = ([fields.vem(3 * part + c, place, tile) for c in range(3)] for part in (1, 2))
            v = solved(place, tile)
            for c in range(3):
                z = v[c] + e[c] * p + m[c] * total
                if inside:
                    zo_ref[c, place] = z
                    z = own.mask * z
                z_ref[c, 2 * place + tile] = z
    for place in range(4):
        own = owns(place)
        fluxes = [flux(lambda i, t, c=c: z_ref[c, 2 * i + t], fields.trans, place, (0,))[0] for c in range(3)]
        z = [zo_ref[c, place] for c in range(3)]
        for c in range(3):
            direct = own.block[c][0] * z[0] + own.block[c][1] * z[1] + own.block[c][2] * z[2]
            total = fluxes[0] if c == 0 else fluxes[0] + fluxes[c]
            w_ref[c, place] = own.mask * (direct - own.mobility[c] * total) + own.rest * z[c]


def first_kernel(
    group, right_ref, block_ref, mobility_ref, trans_ref, mask_ref, cell_ref, columns_ref,
    xn_ref, xp_ref, cn_ref, cp_ref, yn_ref, yp_ref, slots_ref,
    zo_ref, w_ref, fore_ref, back_ref, terms_ref, source_ref, solved_ref,
    p_ref, q_ref, z_ref, scratch_ref, kappa_ref,
):
    @functools.cache
    def owns(place):
        return Own(place, block_ref, mobility_ref, mask_ref)

    def right(place):
        return [right_ref[c, place] for c in range(3)]

    for place in range(4):
        own = owns(place)
        r = right(place)
        kappa_ref[place] = own.kappa()
        source_ref[place] = own.scale * (r[0] + r[1] + r[2])
        v = own.solve(r)
        for c in range(3):
            solved_ref[c, place] = v[c]
    fields = Fields(
        trans_ref, xn_ref, xp_ref, cn_ref, cp_ref, yn_ref, yp_ref,
        lambda k, place: kappa_ref[place] if k == 6 else source_ref[place],
    )

    def solved(place, tile):
        if place < 4 and tile == 0:
            return [solved_ref[c, place] for c in range(3)]
        return [fields.vem(c, place, tile) for c in range(3)]

    application(
        group, fields, slots_ref, lambda place: cell_code(place, mask_ref, cell_ref),
        lambda place, tile: fields.field(7, place, tile), solved, owns, p_ref, q_ref, z_ref, zo_ref, w_ref,
    )
    for place in range(4):
        own = owns(place)
        w = [w_ref[c, place] for c in range(3)]
        source = own.scale * (w[0] + w[1] + w[2])
        v = [own.mask * part for part in own.solve(w)]
        source_ref[place] = source
        for c in range(3):
            solved_ref[c, place] = v[c]
        for out_ref, distance in ((fore_ref, 4 - place), (back_ref, place + 1)):
            if distance < 4:
                put(out_ref, X2_S + distance - 1, source)
            if distance == 1:
                for c in range(3):
                    put(out_ref, c, v[c])
    sums = coarse_sums(cell_ref, lambda i: w_ref[0, i] + w_ref[1, i] + w_ref[2, i])
    terms = coarse_terms(sums, columns_ref, scratch_ref, group)
    terms_ref[...] = terms
    for out_ref in (fore_ref, back_ref):
        out_ref[8 * X2_COARSE :, :128] = terms
        out_ref[8 * X2_COARSE :, 128:] = jnp.zeros((16, 128), F32)


def second_kernel(
    group, right_ref, block_ref, mobility_ref, trans_ref, mask_ref, cell_ref,
    xn_ref, xp_ref, cn_ref, cp_ref, yn_ref, yp_ref, slots_ref, w1_ref, source_ref, xn2_ref, xp2_ref, yn2_ref, yp2_ref,
    zo_ref, sums_ref,
    w_ref, p_ref, q_ref, z_ref, kappa_ref,
):
    @functools.cache
    def owns(place):
        return Own(place, block_ref, mobility_ref, mask_ref)

    for place in range(4):
        kappa_ref[place] = owns(place).kappa()
    fields = Fields(trans_ref, xn_ref, xp_ref, cn_ref, cp_ref, yn_ref, yp_ref, lambda k, place: kappa_ref[place])

    def source(place, tile):
        if tile:
            at = Y2_PLACES.index(place)
            return halo_tile(get(yn2_ref, at // 2), get(yp2_ref, at // 2), at % 2)
        if place < 4:
            return source_ref[place]
        return get(xn2_ref, X2_S + place - 4) if place < 8 else get(xp2_ref, X2_S + 11 - place)

    def solved(place, tile):
        if tile:
            spots = [8 * Y2_V + 4 * c + place for c in range(3)]
            return [edge_rows(yn2_ref, yp2_ref, spot, spot) for spot in spots]
        if place < 4:
            return owns(place).solve([w1_ref[c, place] for c in range(3)])
        return [get(xn2_ref if place == 4 else xp2_ref, c) for c in range(3)]

    application(
        group, fields, slots_ref, lambda place: cell_code(place, mask_ref, cell_ref),
        source, solved, owns, p_ref, q_ref, z_ref, zo_ref, w_ref,
    )
    lane = lax.broadcasted_iota(jnp.int32, (1, 128), 1)
    totals = [jnp.zeros((ROWS, 256), F32) for _ in range(5)]
    for place in range(4):
        for c in range(3):
            a, b, r = w1_ref[c, place], w_ref[c, place], right_ref[c, place]
            for i, term in enumerate((a * a, a * b, b * b, a * r, b * r)):
                totals[i] = totals[i] + term
    line = jnp.zeros((1, 128), F32)
    for i in range(5):
        value = jnp.sum(jnp.sum(totals[i], axis=0, keepdims=True), axis=1, keepdims=True)
        line = line + jnp.where(lane == i, jnp.broadcast_to(value, (1, 128)), 0.0)
    sums_ref[...] = jnp.broadcast_to(line[None], sums_ref.shape)


def regroup_kernel(parts_ref, sums_ref):
    line = jnp.sum(parts_ref[...], axis=0)
    sums_ref[...] = jnp.broadcast_to(line[None], sums_ref.shape)


def combine_kernel(parts_ref, z1_ref, z2_ref, out_ref):
    line = jnp.sum(parts_ref[...], axis=0)
    g11, g12, g22, h1, h2 = [line[:, i : i + 1] for i in range(5)]
    determinant = g11 * g22 - g12 * g12
    c1 = jnp.broadcast_to((g22 * h1 - g12 * h2) / determinant, (ROWS, 256))
    c2 = jnp.broadcast_to((g11 * h2 - g12 * h1) / determinant, (ROWS, 256))
    for c in range(3):
        for place in range(XO):
            out_ref[c, place] = c1 * z1_ref[c, place] + c2 * z2_ref[c, place]


class Sent:
    def __init__(self, axis, tiles, swap=False):
        self.axis, self.shape, self.swap = axis, (8 * tiles, 256), swap

    def exchanged(self, pair):
        count = lax.axis_size(self.axis)
        if self.swap:
            links = [[(i, i + 1) for i in range(start, count - 1, 2)] for start in (1, 0)]
            links = [way + [(j, i) for i, j in way] for way in links]
            second = lax.ppermute(pair[1], self.axis, links[1])
            first = lax.ppermute(pair[0], self.axis, links[0])
            return Received(self.axis, (first, second), True)
        from_previous = lax.ppermute(pair[0], self.axis, [(i, i + 1) for i in range(count - 1)])
        from_next = lax.ppermute(pair[1], self.axis, [(i + 1, i) for i in range(count - 1)])
        return Received(self.axis, (from_next, from_previous), False)


class Received:
    def __init__(self, axis, pair, swap):
        self.axis, self.pair, self.swap = axis, pair, swap


def copied(axis, even, odd):
    def body(pairs):
        def copy():
            for from_ref, to_ref in pairs:
                to_ref[...] = from_ref[...]

        return copy

    is_odd = lax.axis_index(axis) % 2
    pl.when(is_odd == 1)(body(odd))
    pl.when(is_odd == 0)(body(even))


def call(kernel, outs, scratch, *args, smem=0, space=pltpu.VMEM):
    vmem = pl.BlockSpec(memory_space=pltpu.VMEM)
    flat, specs, shapes, views = [], [], [], []
    for i, arg in enumerate(args):
        parts = arg.pair if isinstance(arg, Received) else [arg]
        flat += parts
        specs += [pl.BlockSpec(memory_space=pltpu.SMEM if i < smem else space)] * len(parts)
        if isinstance(arg, Received) and arg.swap:
            views += [arg.pair[0].shape] * 2
    for out in outs:
        shapes += [out.shape] * 2 if isinstance(out, Sent) else [out]
        if isinstance(out, Sent) and out.swap:
            views += [out.shape] * 2

    def body(*refs):
        refs = list(refs)
        ins, results = refs[: len(flat)], refs[len(flat) : len(flat) + len(shapes)]
        copies = refs[len(flat) + len(shapes) : len(flat) + len(shapes) + len(views)]
        rest = refs[len(flat) + len(shapes) + len(views) :]
        seen, after = [], []
        for arg in args:
            parts = [ins.pop(0) for _ in range(2 if isinstance(arg, Received) else 1)]
            if isinstance(arg, Received) and arg.swap:
                first, second = parts
                parts = ahead, behind = copies.pop(0), copies.pop(0)
                copied(arg.axis, [(second, ahead), (first, behind)], [(first, ahead), (second, behind)])
            seen += parts
        for out in outs:
            parts = [results.pop(0) for _ in range(2 if isinstance(out, Sent) else 1)]
            if isinstance(out, Sent) and out.swap:
                first, second = parts
                parts = ahead, behind = copies.pop(0), copies.pop(0)
                after.append((out.axis, [(ahead, second), (behind, first)], [(ahead, first), (behind, second)]))
            seen += parts
        kernel(*seen, *rest)
        for each in after:
            copied(*each)

    found = list(
        pl.pallas_call(
            body,
            out_shape=[jax.ShapeDtypeStruct(shape, F32) for shape in shapes],
            in_specs=specs,
            out_specs=[vmem] * len(shapes),
            scratch_shapes=[pltpu.VMEM(shape, F32) for shape in views]
            + [pltpu.VMEM(shape, F32) if isinstance(shape, tuple) else shape for shape in scratch],
            compiler_params=pltpu.CompilerParams(vmem_limit_bytes=40 * 2**20),
        )(*flat)
    )
    results = []
    for out in outs:
        if isinstance(out, Sent):
            results.append(out.exchanged([found.pop(0), found.pop(0)]))
        else:
            results.append(found.pop(0))
    return results


def on_device(
    right_side, block_matrix, mobility, trans, active_mask, cell_map, coarse_owner, coarse_rows
):
    group = lax.axis_size("gy")
    line = lax.axis_size("gx")
    local = (right_side, block_matrix, mobility, trans, active_mask, cell_map)
    field = (3, XO, ROWS, 256)
    columns, y_halos, x_halos = call(
        functools.partial(pack_kernel, group),
        [(group, 1, 64 * NC + 128), Sent("gy", Y_TILES, True), Sent("gx", X_TILES, True)],
        [(ROWS, 256), coarse_rows.shape]
        + [pltpu.VMEM(arg.shape, arg.dtype) for arg in local]
        + [pltpu.SemaphoreType.DMA((7,))],
        coarse_owner, *[pltpu.with_memory_space_constraint(arg, pltpu.HBM) for arg in (coarse_rows, *local)],
        smem=1, space=pltpu.HBM,
    )
    columns = lax.all_to_all(columns, "gy", 0, 0)
    corners, terms = call(
        functools.partial(sides_kernel, group),
        [Sent("gx", C_TILES, True), (16, 128)],
        [(16, 128)],
        right_side, cell_map, columns, y_halos,
    )
    (slots,) = call(functools.partial(slots_kernel, group), [(group, 1, 768)], [], terms, corners)
    slots = lax.all_to_all(slots, "gy", 0, 0)
    halos = (x_halos, corners, y_halos)
    work = [(24, ROWS, 256), (24, ROWS, 256), (3, 24, ROWS, 256)]
    first_z, first_w, x2_halos, terms, source, solved = call(
        functools.partial(first_kernel, group),
        [field, field, Sent("gx", X2_TILES, True), (16, 128), (XO, ROWS, 256), field],
        work + [(16, 128), (XO, ROWS, 256)],
        *local, columns, *halos, slots,
    )
    slots, y2_halos = call(
        functools.partial(forward_kernel, group),
        [(group, 1, 768), Sent("gy", Y2_TILES, True)],
        [],
        terms, source, solved, x2_halos,
    )
    slots = lax.all_to_all(slots, "gy", 0, 0)
    second_z, sums = call(
        functools.partial(second_kernel, group),
        [field, (line, 1, 128)],
        [field] + work + [(XO, ROWS, 256)],
        *local, *halos, slots, first_w, source, x2_halos, y2_halos,
    )
    sums = lax.all_to_all(sums, "gx", 0, 0)
    (sums,) = call(regroup_kernel, [(group, 1, 128)], [], sums)
    sums = lax.all_to_all(sums, "gy", 0, 0)
    return call(combine_kernel, [field], [], sums, first_z, second_z)[0]


def solution(mesh):
    in_specs = (
        P(None, "gx", "gy", None),
        P(None, None, "gx", "gy", None),
        P(None, "gx", "gy", None),
        P(None, "gx", "gy", None),
        P("gx", "gy", None),
        P("gx", "gy", None),
        P("gx", "gy"),
        P(("gx", "gy"), None),
    )
    out_specs = P(None, "gx", "gy", None)
    return jax.shard_map(
        on_device, mesh=mesh, in_specs=in_specs, out_specs=out_specs, check_vma=False
    )
```

```python
import functools

import jax
import jax.numpy as jnp
from jax import lax
from jax.experimental import pallas as pl
from jax.experimental.pallas import tpu as pltpu
from jax.sharding import PartitionSpec as P

DAMPING = 0.8
F32 = jnp.float32
XO = 4
ROWS = 8
NC = 64

X_FIELD, X_VEM, X_TILES = 4, 28, 37
C_CELL13, C_CELL2, C_COARSE, C_TILES = 8, 9, 10, 11
Y_FIELD, Y_LAST, Y_TILES = 2, 18, 19
X2_S, X2_COARSE, X2_TILES = 3, 6, 7
Y2_V, Y2_TILES = 4, 6
Y2_PLACES = (0, 1, 2, 3, 4, 5, 10, 11)


def row_index():
    return lax.broadcasted_iota(jnp.int32, (ROWS, 256), 0)


def turned(tile, by):
    return pltpu.roll(tile, by, axis=0)


def put(ref, index, tile):
    ref[8 * index : 8 * index + 8, :] = tile


def get(ref, index):
    return ref[8 * index : 8 * index + 8, :]


class Own:
    def __init__(self, place, block_ref, mobility_ref, mask_ref):
        self.mask = mask = mask_ref[place].astype(F32)
        self.rest = rest = 1.0 - mask
        self.block = [[block_ref[c, j, place] for j in range(3)] for c in range(3)]
        self.mobility = [mobility_ref[c, place] for c in range(3)]
        e = [
            [mask * self.block[c][j] + rest if c == j else mask * self.block[c][j] for j in range(3)]
            for c in range(3)
        ]
        cof = [
            [
                e[(c + 1) % 3][(j + 1) % 3] * e[(c + 2) % 3][(j + 2) % 3]
                - e[(c + 1) % 3][(j + 2) % 3] * e[(c + 2) % 3][(j + 1) % 3]
                for j in range(3)
            ]
            for c in range(3)
        ]
        recip = 1.0 / (e[0][0] * cof[0][0] + e[0][1] * cof[0][1] + e[0][2] * cof[0][2])
        self.inverse = [[cof[j][c] * recip for j in range(3)] for c in range(3)]
        self.entry = e
        self.scale = DAMPING * mask / (mask * (self.block[0][0] + self.block[1][0] + self.block[2][0]) + rest)

    def solve(self, vector):
        i = self.inverse
        return [i[c][0] * vector[0] + i[c][1] * vector[1] + i[c][2] * vector[2] for c in range(3)]

    def kappa(self):
        return self.scale * (self.mobility[0] + self.mobility[1] + self.mobility[2])

    def of_pressure(self):
        column = self.solve([self.entry[j][0] for j in range(3)])
        return [1.0 - column[0], -column[1], -column[2]]

    def of_flux(self):
        return self.solve([self.mask * self.mobility[j] for j in range(3)])


def cell_code(place, mask_ref, cell_ref):
    return jnp.where(mask_ref[place] > 0, cell_ref[place], -1).astype(F32)


def coarse_sums(cell_ref, of_row):
    wanted = lax.broadcasted_iota(jnp.int32, (NC, 256), 0)
    total = jnp.zeros((NC, 256), F32)
    for place in range(XO):
        cells, values = cell_ref[place], of_row(place)
        for row in range(ROWS):
            here = jnp.broadcast_to(cells[row : row + 1], (NC, 256)) == wanted
            total = total + jnp.where(here, jnp.broadcast_to(values[row : row + 1], (NC, 256)), 0.0)
    return jnp.sum(total[:, :128] + total[:, 128:], axis=1, keepdims=True)


def segment(ref, j, k):
    return ref[j, :, 128 * k : 128 * k + 128]


def coarse_terms(sums, columns_ref, terms_ref, group):
    lane = lax.broadcasted_iota(jnp.int32, (NC // 2, 128), 1)
    weights = jnp.where(
        lane < NC,
        jnp.broadcast_to(sums[: NC // 2], (NC // 2, 128)),
        jnp.broadcast_to(sums[NC // 2 :], (NC // 2, 128)),
    )
    result = jnp.zeros(terms_ref.shape, F32)
    for j in range(group):
        terms_ref[j : j + 1, :] = segment(columns_ref, j, NC // 2)
    owners = terms_ref[...]
    for j in range(group):
        line = segment(columns_ref, j, 0) * weights[:1]
        for k in range(1, NC // 2):
            line = line + segment(columns_ref, j, k) * weights[k : k + 1]
        line = line + pltpu.roll(line, NC, axis=1)
        result = result + jnp.where(owners == float(j), jnp.broadcast_to(line, result.shape), 0.0)
    return result


def shifted_lanes(tile):
    lane = lax.broadcasted_iota(jnp.int32, (ROWS, 256), 1)
    after = jnp.where(lane < 255, pltpu.roll(tile, 255, axis=1), 0.0)
    before = jnp.where(lane > 0, pltpu.roll(tile, 1, axis=1), 0.0)
    return after, before


def flux(field, trans, place, tiles):
    own, halo = field(place, 0), field(place, 1)
    inner = row_index() < 7
    outer = row_index() > 0
    own_up, halo_up, own_down, halo_down = turned(own, 7), turned(halo, 7), turned(own, 1), turned(halo, 1)
    result = []
    for tile in tiles:
        if tile == 0:
            up, down = jnp.where(inner, own_up, halo_up), jnp.where(outer, own_down, halo_down)
        else:
            up, down = jnp.where(inner, halo_up, own_up), jnp.where(outer, halo_down, own_down)
        after, before = shifted_lanes(halo if tile else own)
        total = trans(0, place, tile) * field((place + 1) % 12, tile)
        total = total + trans(1, place, tile) * field((place + 11) % 12, tile)
        total = total + trans(2, place, tile) * up
        total = total + trans(3, place, tile) * down
        total = total + trans(4, place, tile) * after
        total = total + trans(5, place, tile) * before
        result.append(total)
    return result


def paired(tiles, to_next):
    first, second = tiles
    low = row_index() < 4
    if to_next:
        return jnp.where(low, turned(first, 4), second)
    return jnp.where(low, first, turned(second, 4))


def halo_tile(next_pair, previous_pair, which):
    low = row_index() < 4
    if which == 0:
        return jnp.where(low, next_pair, turned(previous_pair, 4))
    return jnp.where(low, turned(next_pair, 4), previous_pair)


def pack_kernel(
    group, owner_ref, rows_hbm, right_hbm, block_hbm, mobility_hbm, trans_hbm, mask_hbm, cell_hbm,
    columns_ref, up_ref, down_ref, fore_ref, back_ref,
    field_ref, rows_ref, right_ref, block_ref, mobility_ref, trans_ref, mask_ref, cell_ref, sems,
):
    pairs = (
        (rows_hbm, rows_ref), (block_hbm, block_ref), (right_hbm, right_ref), (mobility_hbm, mobility_ref),
        (trans_hbm, trans_ref), (mask_hbm, mask_ref), (cell_hbm, cell_ref),
    )
    copies = [pltpu.make_async_copy(a, b, sems.at[i]) for i, (a, b) in enumerate(pairs)]
    for copy in copies:
        copy.start()
    copies[0].wait()
    lane = lax.broadcasted_iota(jnp.int32, (NC // 2, 128), 1)
    owner = jnp.full((1, 128), owner_ref[0, 0], jnp.int32).astype(F32)
    for pair in range(group // 2):
        part = rows_ref[:, 128 * pair : 128 * pair + 128]
        flipped = jnp.concatenate([part, part], axis=0).T
        for odd in range(2):
            block = flipped[NC * odd : NC * odd + NC]
            block = jnp.where(lane < NC, block[: NC // 2], block[NC // 2 :])
            for k in range(NC // 2):
                columns_ref[2 * pair + odd, :, 128 * k : 128 * k + 128] = block[k : k + 1]
            columns_ref[2 * pair + odd, :, 64 * NC :] = owner
    for copy in copies[1:]:
        copy.wait()
    for out_ref in (up_ref, down_ref):
        out_ref[8 * Y_TILES - 4 :, :] = jnp.zeros((4, 256), F32)
    for half in range(2):
        cells, fields, edges = [], [], []
        for place in (2 * half, 2 * half + 1):
            own = Own(place, block_ref, mobility_ref, mask_ref)
            cells.append(cell_code(place, mask_ref, cell_ref))
            right = [right_ref[c, place] for c in range(3)]
            fields.append(
                [trans_ref[face, place] for face in range(6)]
                + [own.kappa(), own.scale * (right[0] + right[1] + right[2])]
            )
            vem = [own.mask * v for v in own.solve(right)] + own.of_pressure() + own.of_flux()
            for out_ref, distance in ((fore_ref, 4 - place), (back_ref, place + 1)):
                put(out_ref, distance - 1, cells[-1])
                if distance < 4:
                    for k in range(8):
                        put(out_ref, X_FIELD + 3 * k + distance - 1, fields[-1][k])
                if distance == 1:
                    for f in range(9):
                        put(out_ref, X_VEM + f, vem[f])
            edges.append(vem)
        for out_ref, to_next in ((up_ref, True), (down_ref, False)):
            put(out_ref, half, paired(cells, to_next))
            free = row_index() % 4 == (0 if to_next else 3)
            for k in range(8):
                edge = [turned(edges[0][k], 1 if to_next else 3), turned(edges[1][k], 5 if to_next else 7)]
                both = jnp.where(row_index() < 4, edge[0], edge[1])
                put(out_ref, Y_FIELD + 2 * k + half, jnp.where(free, both, paired([fields[0][k], fields[1][k]], to_next)))
            for i in range(2):
                field_ref[...] = edges[i][8]
                spot = 8 * Y_LAST + 2 * half + i
                out_ref[spot : spot + 1, :] = field_ref[7:8, :] if to_next else field_ref[0:1, :]


def y_halo(next_ref, previous_ref, index, place):
    at = index + place // 2
    return halo_tile(get(next_ref, at), get(previous_ref, at), place % 2)


def sides_kernel(
    group, right_ref, cell_ref, columns_ref, yn_ref, yp_ref,
    fore_ref, back_ref, terms_ref, scratch_ref,
):
    row = row_index()
    middle = (row == 3) | (row == 4)
    sums = coarse_sums(cell_ref, lambda i: right_ref[0, i] + right_ref[1, i] + right_ref[2, i])
    terms = coarse_terms(sums, columns_ref, scratch_ref, group)
    terms_ref[...] = terms
    for out_ref, at in ((fore_ref, lambda d: 4 - d), (back_ref, lambda d: d - 1)):
        for k in range(8):
            near, far = [y_halo(yn_ref, yp_ref, Y_FIELD + 2 * k, at(d)) for d in (1, 2)]
            put(out_ref, k, jnp.where(middle, turned(far, 4), near))
        near, mid, far = [y_halo(yn_ref, yp_ref, 0, at(d)) for d in (1, 2, 3)]
        put(out_ref, C_CELL13, jnp.where(middle, turned(far, 4), near))
        put(out_ref, C_CELL2, mid)
        out_ref[8 * C_COARSE :, :128] = terms[:8]
        out_ref[8 * C_COARSE :, 128:] = terms[8:]


def write_slots(group, slots_ref, three):
    lane = lax.broadcasted_iota(jnp.int32, (1, 128), 1)
    zero = jnp.zeros((1, 128), F32)
    for b in range(group):
        for i, line in enumerate(three):
            after = line(b + 1) if b + 1 < group else zero
            before = line(b - 1) if b > 0 else zero
            slots_ref[b, :, 128 * i : 128 * i + 128] = line(b)
            slots_ref[b, :, 128 * i + 384 : 128 * i + 512] = jnp.where(lane < NC, after, before)


def three_groups(terms_ref, next_ref, previous_ref, start):
    return (
        lambda b: terms_ref[b : b + 1, :],
        lambda b: next_ref[start + b % 8 : start + b % 8 + 1, 128 * (b // 8) : 128 * (b // 8) + 128],
        lambda b: previous_ref[start + b % 8 : start + b % 8 + 1, 128 * (b // 8) : 128 * (b // 8) + 128],
    )


def slots_kernel(group, terms_ref, next_ref, previous_ref, slots_ref):
    write_slots(group, slots_ref, three_groups(terms_ref, next_ref, previous_ref, 8 * C_COARSE))


def forward_kernel(group, terms_ref, source_ref, solved_ref, next_ref, previous_ref, slots_ref, up_ref, down_ref):
    write_slots(group, slots_ref, three_groups(terms_ref, next_ref, previous_ref, 8 * X2_COARSE))

    def source(place):
        if place < 4:
            return source_ref[place]
        return get(next_ref, X2_S + place - 4) if place < 8 else get(previous_ref, X2_S + 11 - place)

    for out_ref, to_next in ((up_ref, True), (down_ref, False)):
        for half in range(4):
            put(out_ref, half, paired([source(Y2_PLACES[2 * half]), source(Y2_PLACES[2 * half + 1])], to_next))
        out_ref[8 * Y2_TILES - 4 :, :] = jnp.zeros((4, 256), F32)
        edge = 7 if to_next else 0
        for f in range(3):
            for place in range(XO):
                spot = 8 * Y2_V + 4 * f + place
                out_ref[spot : spot + 1, :] = solved_ref[f, place, edge : edge + 1, :]


class Fields:
    def __init__(self, trans_ref, xn_ref, xp_ref, cn_ref, cp_ref, yn_ref, yp_ref, own):
        self.trans_ref, self.own = trans_ref, own
        self.x, self.corner, self.y = (xn_ref, xp_ref), (cn_ref, cp_ref), (yn_ref, yp_ref)

    def side(self, place, tile):
        refs = self.corner if tile else self.x
        return (refs[0], place - 3) if place < 8 else (refs[1], 12 - place)

    def field(self, k, place, tile):
        if place < 4:
            if tile:
                return y_halo(self.y[0], self.y[1], Y_FIELD + 2 * k, place)
            return self.trans_ref[k, place] if k < 6 else self.own(k, place)
        ref, d = self.side(place, tile)
        if tile == 0:
            return get(ref, X_FIELD + 3 * k + d - 1)
        corner = get(ref, k)
        return corner if d == 1 else turned(corner, 4)

    def trans(self, face, place, tile):
        return self.field(face, place, tile)

    def cells(self, place, tile, own_cells):
        if place < 4:
            return y_halo(self.y[0], self.y[1], 0, place) if tile else own_cells(place)
        ref, d = self.side(place, tile)
        if tile == 0:
            return get(ref, d - 1)
        if d == 2:
            return get(ref, C_CELL2)
        corner = get(ref, C_CELL13)
        return corner if d == 1 else turned(corner, 4)

    def vem(self, f, place, tile):
        if tile == 0:
            return get(self.x[0] if place == 4 else self.x[1], X_VEM + f)
        if f == 8:
            return edge_rows(self.y[0], self.y[1], 8 * Y_LAST + place, 8 * Y_LAST + place)
        spot = 8 * (Y_FIELD + 2 * f + place // 2) + 4 * (place % 2)
        return edge_rows(self.y[0], self.y[1], spot + 3, spot)


def edge_rows(next_ref, previous_ref, next_spot, previous_spot):
    after = jnp.broadcast_to(next_ref[next_spot : next_spot + 1, :], (ROWS, 256))
    before = jnp.broadcast_to(previous_ref[previous_spot : previous_spot + 1, :], (ROWS, 256))
    return jnp.where(row_index() < 4, after, before)


def picked(coarse, code, tile, group):
    index = jnp.maximum(code, 0.0).astype(jnp.int32)
    if tile:
        index = index + jnp.where(row_index() < 4, 0, NC)
    line = 3 * tile + group
    table = jnp.broadcast_to(coarse[:, 128 * line : 128 * line + 128], (ROWS, 128))
    found = [jnp.take_along_axis(table, index[:, 128 * h : 128 * h + 128], axis=1) for h in range(2)]
    return jnp.where(code >= 0.0, jnp.concatenate(found, axis=1), 0.0)


def application(group, fields, slots_ref, own_cells, source, solved, owns, p_ref, q_ref, z_ref, zo_ref, w_ref):
    coarse = slots_ref[0]
    for b in range(1, group):
        coarse = coarse + slots_ref[b]
    for place in range(12):
        for tile in range(2):
            if tile and place in (7, 8):
                continue
            code = fields.cells(place, tile, own_cells)
            p_ref[2 * place + tile] = picked(coarse, code, tile, (place >= 4) + (place >= 8))

    def sweep(from_ref, to_ref, both, single):
        def pressure(place, tile):
            return from_ref[2 * place + tile]

        for place in both + single:
            tiles = (0, 1) if place in both else (0,)
            for tile, total in zip(tiles, flux(pressure, fields.trans, place, tiles), strict=True):
                to_ref[2 * place + tile] = (
                    (1.0 - DAMPING) * pressure(place, tile)
                    + source(place, tile)
                    + fields.field(6, place, tile) * total
                )

    sweep(p_ref, q_ref, (0, 1, 2, 3, 4, 5, 10, 11), (6, 9))
    sweep(q_ref, p_ref, (0, 1, 2, 3, 4, 11), (5, 10))

    def pressure(place, tile):
        return p_ref[2 * place + tile]

    for place in (0, 1, 2, 3, 4, 11):
        tiles = (0, 1) if place < 4 else (0,)
        for tile, total in zip(tiles, flux(pressure, fields.trans, place, tiles), strict=True):
            p = pressure(place, tile)
            inside = place < 4 and tile == 0
            if inside:
                own = owns(place)
                e, m = own.of_pressure(), own.of_flux()
            else:
                e, m = ([fields.vem(3 * part + c, place, tile) for c in range(3)] for part in (1, 2))
            v = solved(place, tile)
            for c in range(3):
                z = v[c] + e[c] * p + m[c] * total
                if inside:
                    zo_ref[c, place] = z
                    z = own.mask * z
                z_ref[c, 2 * place + tile] = z
    for place in range(4):
        own = owns(place)
        fluxes = [flux(lambda i, t, c=c: z_ref[c, 2 * i + t], fields.trans, place, (0,))[0] for c in range(3)]
        z = [zo_ref[c, place] for c in range(3)]
        for c in range(3):
            direct = own.block[c][0] * z[0] + own.block[c][1] * z[1] + own.block[c][2] * z[2]
            total = fluxes[0] if c == 0 else fluxes[0] + fluxes[c]
            w_ref[c, place] = own.mask * (direct - own.mobility[c] * total) + own.rest * z[c]


def first_kernel(
    group, right_ref, block_ref, mobility_ref, trans_ref, mask_ref, cell_ref, columns_ref,
    xn_ref, xp_ref, cn_ref, cp_ref, yn_ref, yp_ref, slots_ref,
    zo_ref, w_ref, fore_ref, back_ref, terms_ref, source_ref, solved_ref,
    p_ref, q_ref, z_ref, scratch_ref, kappa_ref,
):
    @functools.cache
    def owns(place):
        return Own(place, block_ref, mobility_ref, mask_ref)

    def right(place):
        return [right_ref[c, place] for c in range(3)]

    for place in range(4):
        own = owns(place)
        r = right(place)
        kappa_ref[place] = own.kappa()
        source_ref[place] = own.scale * (r[0] + r[1] + r[2])
        v = own.solve(r)
        for c in range(3):
            solved_ref[c, place] = v[c]
    fields = Fields(
        trans_ref, xn_ref, xp_ref, cn_ref, cp_ref, yn_ref, yp_ref,
        lambda k, place: kappa_ref[place] if k == 6 else source_ref[place],
    )

    def solved(place, tile):
        if place < 4 and tile == 0:
            return [solved_ref[c, place] for c in range(3)]
        return [fields.vem(c, place, tile) for c in range(3)]

    application(
        group, fields, slots_ref, lambda place: cell_code(place, mask_ref, cell_ref),
        lambda place, tile: fields.field(7, place, tile), solved, owns, p_ref, q_ref, z_ref, zo_ref, w_ref,
    )
    for place in range(4):
        own = owns(place)
        w = [w_ref[c, place] for c in range(3)]
        source = own.scale * (w[0] + w[1] + w[2])
        v = [own.mask * part for part in own.solve(w)]
        source_ref[place] = source
        for c in range(3):
            solved_ref[c, place] = v[c]
        for out_ref, distance in ((fore_ref, 4 - place), (back_ref, place + 1)):
            if distance < 4:
                put(out_ref, X2_S + distance - 1, source)
            if distance == 1:
                for c in range(3):
                    put(out_ref, c, v[c])
    sums = coarse_sums(cell_ref, lambda i: w_ref[0, i] + w_ref[1, i] + w_ref[2, i])
    terms = coarse_terms(sums, columns_ref, scratch_ref, group)
    terms_ref[...] = terms
    for out_ref in (fore_ref, back_ref):
        out_ref[8 * X2_COARSE :, :128] = terms[:8]
        out_ref[8 * X2_COARSE :, 128:] = terms[8:]


def second_kernel(
    group, right_ref, block_ref, mobility_ref, trans_ref, mask_ref, cell_ref,
    xn_ref, xp_ref, cn_ref, cp_ref, yn_ref, yp_ref, slots_ref, w1_ref, source_ref, xn2_ref, xp2_ref, yn2_ref, yp2_ref,
    zo_ref, sums_ref,
    w_ref, p_ref, q_ref, z_ref, kappa_ref,
):
    @functools.cache
    def owns(place):
        return Own(place, block_ref, mobility_ref, mask_ref)

    for place in range(4):
        kappa_ref[place] = owns(place).kappa()
    fields = Fields(trans_ref, xn_ref, xp_ref, cn_ref, cp_ref, yn_ref, yp_ref, lambda k, place: kappa_ref[place])

    def source(place, tile):
        if tile:
            at = Y2_PLACES.index(place)
            return halo_tile(get(yn2_ref, at // 2), get(yp2_ref, at // 2), at % 2)
        if place < 4:
            return source_ref[place]
        return get(xn2_ref, X2_S + place - 4) if place < 8 else get(xp2_ref, X2_S + 11 - place)

    def solved(place, tile):
        if tile:
            spots = [8 * Y2_V + 4 * c + place for c in range(3)]
            return [edge_rows(yn2_ref, yp2_ref, spot, spot) for spot in spots]
        if place < 4:
            return owns(place).solve([w1_ref[c, place] for c in range(3)])
        return [get(xn2_ref if place == 4 else xp2_ref, c) for c in range(3)]

    application(
        group, fields, slots_ref, lambda place: cell_code(place, mask_ref, cell_ref),
        source, solved, owns, p_ref, q_ref, z_ref, zo_ref, w_ref,
    )
    lane = lax.broadcasted_iota(jnp.int32, (1, 128), 1)
    totals = [jnp.zeros((ROWS, 256), F32) for _ in range(5)]
    for place in range(4):
        for c in range(3):
            a, b, r = w1_ref[c, place], w_ref[c, place], right_ref[c, place]
            for i, term in enumerate((a * a, a * b, b * b, a * r, b * r)):
                totals[i] = totals[i] + term
    line = jnp.zeros((1, 128), F32)
    for i in range(5):
        value = jnp.sum(jnp.sum(totals[i], axis=0, keepdims=True), axis=1, keepdims=True)
        line = line + jnp.where(lane == i, jnp.broadcast_to(value, (1, 128)), 0.0)
    sums_ref[...] = jnp.broadcast_to(line[None], sums_ref.shape)


def regroup_kernel(parts_ref, sums_ref):
    line = jnp.sum(parts_ref[...], axis=0)
    sums_ref[...] = jnp.broadcast_to(line[None], sums_ref.shape)


def combine_kernel(parts_ref, z1_ref, z2_ref, out_ref):
    line = jnp.sum(parts_ref[...], axis=0)
    g11, g12, g22, h1, h2 = [line[:, i : i + 1] for i in range(5)]
    determinant = g11 * g22 - g12 * g12
    c1 = jnp.broadcast_to((g22 * h1 - g12 * h2) / determinant, (ROWS, 256))
    c2 = jnp.broadcast_to((g11 * h2 - g12 * h1) / determinant, (ROWS, 256))
    for c in range(3):
        for place in range(XO):
            out_ref[c, place] = c1 * z1_ref[c, place] + c2 * z2_ref[c, place]


class Sent:
    def __init__(self, axis, tiles, swap=False):
        self.axis, self.shape, self.swap = axis, (8 * tiles, 256), swap

    def exchanged(self, pair):
        count = lax.axis_size(self.axis)
        if self.swap:
            links = [[(i, i + 1) for i in range(start, count - 1, 2)] for start in (1, 0)]
            links = [way + [(j, i) for i, j in way] for way in links]
            second = lax.ppermute(pair[1], self.axis, links[1])
            first = lax.ppermute(pair[0], self.axis, links[0])
            return Received(self.axis, (first, second), True)
        from_previous = lax.ppermute(pair[0], self.axis, [(i, i + 1) for i in range(count - 1)])
        from_next = lax.ppermute(pair[1], self.axis, [(i + 1, i) for i in range(count - 1)])
        return Received(self.axis, (from_next, from_previous), False)


class Received:
    def __init__(self, axis, pair, swap):
        self.axis, self.pair, self.swap = axis, pair, swap


def copied(axis, even, odd):
    def body(pairs):
        def copy():
            for from_ref, to_ref in pairs:
                to_ref[...] = from_ref[...]

        return copy

    is_odd = lax.axis_index(axis) % 2
    pl.when(is_odd == 1)(body(odd))
    pl.when(is_odd == 0)(body(even))


def call(kernel, outs, scratch, *args, smem=0, space=pltpu.VMEM):
    vmem = pl.BlockSpec(memory_space=pltpu.VMEM)
    flat, specs, shapes, views = [], [], [], []
    for i, arg in enumerate(args):
        parts = arg.pair if isinstance(arg, Received) else [arg]
        flat += parts
        specs += [pl.BlockSpec(memory_space=pltpu.SMEM if i < smem else space)] * len(parts)
        if isinstance(arg, Received) and arg.swap:
            views += [arg.pair[0].shape] * 2
    for out in outs:
        shapes += [out.shape] * 2 if isinstance(out, Sent) else [out]
        if isinstance(out, Sent) and out.swap:
            views += [out.shape] * 2

    def body(*refs):
        refs = list(refs)
        ins, results = refs[: len(flat)], refs[len(flat) : len(flat) + len(shapes)]
        copies = refs[len(flat) + len(shapes) : len(flat) + len(shapes) + len(views)]
        rest = refs[len(flat) + len(shapes) + len(views) :]
        seen, after = [], []
        for arg in args:
            parts = [ins.pop(0) for _ in range(2 if isinstance(arg, Received) else 1)]
            if isinstance(arg, Received) and arg.swap:
                first, second = parts
                parts = ahead, behind = copies.pop(0), copies.pop(0)
                copied(arg.axis, [(second, ahead), (first, behind)], [(first, ahead), (second, behind)])
            seen += parts
        for out in outs:
            parts = [results.pop(0) for _ in range(2 if isinstance(out, Sent) else 1)]
            if isinstance(out, Sent) and out.swap:
                first, second = parts
                parts = ahead, behind = copies.pop(0), copies.pop(0)
                after.append((out.axis, [(ahead, second), (behind, first)], [(ahead, first), (behind, second)]))
            seen += parts
        kernel(*seen, *rest)
        for each in after:
            copied(*each)

    found = list(
        pl.pallas_call(
            body,
            out_shape=[jax.ShapeDtypeStruct(shape, F32) for shape in shapes],
            in_specs=specs,
            out_specs=[vmem] * len(shapes),
            scratch_shapes=[pltpu.VMEM(shape, F32) for shape in views]
            + [pltpu.VMEM(shape, F32) if isinstance(shape, tuple) else shape for shape in scratch],
            compiler_params=pltpu.CompilerParams(vmem_limit_bytes=40 * 2**20),
        )(*flat)
    )
    results = []
    for out in outs:
        if isinstance(out, Sent):
            results.append(out.exchanged([found.pop(0), found.pop(0)]))
        else:
            results.append(found.pop(0))
    return results


def on_device(
    right_side, block_matrix, mobility, trans, active_mask, cell_map, coarse_owner, coarse_rows
):
    group = lax.axis_size("gy")
    line = lax.axis_size("gx")
    local = (right_side, block_matrix, mobility, trans, active_mask, cell_map)
    field = (3, XO, ROWS, 256)
    columns, y_halos, x_halos = call(
        functools.partial(pack_kernel, group),
        [(group, 1, 64 * NC + 128), Sent("gy", Y_TILES, True), Sent("gx", X_TILES, True)],
        [(ROWS, 256), coarse_rows.shape]
        + [pltpu.VMEM(arg.shape, arg.dtype) for arg in local]
        + [pltpu.SemaphoreType.DMA((7,))],
        coarse_owner, *[pltpu.with_memory_space_constraint(arg, pltpu.HBM) for arg in (coarse_rows, *local)],
        smem=1, space=pltpu.HBM,
    )
    columns = lax.all_to_all(columns, "gy", 0, 0)
    corners, terms = call(
        functools.partial(sides_kernel, group),
        [Sent("gx", C_TILES, True), (16, 128)],
        [(16, 128)],
        right_side, cell_map, columns, y_halos,
    )
    (slots,) = call(functools.partial(slots_kernel, group), [(group, 1, 768)], [], terms, corners)
    slots = lax.all_to_all(slots, "gy", 0, 0)
    halos = (x_halos, corners, y_halos)
    work = [(24, ROWS, 256), (24, ROWS, 256), (3, 24, ROWS, 256)]
    first_z, first_w, x2_halos, terms, source, solved = call(
        functools.partial(first_kernel, group),
        [field, field, Sent("gx", X2_TILES, True), (16, 128), (XO, ROWS, 256), field],
        work + [(16, 128), (XO, ROWS, 256)],
        *local, columns, *halos, slots,
    )
    slots, y2_halos = call(
        functools.partial(forward_kernel, group),
        [(group, 1, 768), Sent("gy", Y2_TILES, True)],
        [],
        terms, source, solved, x2_halos,
    )
    slots = lax.all_to_all(slots, "gy", 0, 0)
    second_z, sums = call(
        functools.partial(second_kernel, group),
        [field, (line, 1, 128)],
        [field] + work + [(XO, ROWS, 256)],
        *local, *halos, slots, first_w, source, x2_halos, y2_halos,
    )
    sums = lax.all_to_all(sums, "gx", 0, 0)
    (sums,) = call(regroup_kernel, [(group, 1, 128)], [], sums)
    sums = lax.all_to_all(sums, "gy", 0, 0)
    return call(combine_kernel, [field], [], sums, first_z, second_z)[0]


def solution(mesh):
    in_specs = (
        P(None, "gx", "gy", None),
        P(None, None, "gx", "gy", None),
        P(None, "gx", "gy", None),
        P(None, "gx", "gy", None),
        P("gx", "gy", None),
        P("gx", "gy", None),
        P("gx", "gy"),
        P(("gx", "gy"), None),
    )
    out_specs = P(None, "gx", "gy", None)
    return jax.shard_map(
        on_device, mesh=mesh, in_specs=in_specs, out_specs=out_specs, check_vma=False
    )
```
